256 devices in a mesh: mode: 64 (over z, x_lo, y), space: 4 (over x_hi, core).
Axes of the slice: x: 4 (x_hi: 2, x_lo: 2; x = x_hi * 2 + x_lo), y: 4, z: 8, core: 2. Of those that a mesh axis runs over, the one named last changes fastest.
Arguments:
- coefs: bfloat16 [4096, 4, 2, 256], P('mode', 'space'), may hold values from -6 to 6
- counts: int32 [4096, 4], P('mode', 'space'), may hold values from 1 to 256
- route: int32 [4096], replicated, may hold values from 0 to 4095, as said below
- basis: bfloat16 [8, 2, 256, 3072], P('space'), may hold values from -0.046875 to 0.046875
- momenta: int32 [4, 3], replicated, may hold values from -3 to 3
- gammas: int32 [4], replicated, may hold values from 0 to 15
Outputs:
- window: float32 [8, 4, 2, 7, 32, 2048], P('space', None, None, None, None, 'mode')
The draws below stay inside these ranges and needn't reach their ends.
Inputs may be any that keep to these rules, and one draw needn't show every extreme that they name: route is a permutation. The 64 slots of one reader (an aligned block of route, also of coefs and counts) name at most 2 items of any one owner, exactly 2 for 32 owners.
All inputs are finite; a program needn't handle non-finite values.
Results may differ from the reference program's by a relative error of at most 0.0027.
Values may be sent and summed in bfloat16 or wider, within the bound.
No kernel may reach another device: no remote copies, remote signals or barrier semaphores. Data moves between devices by JAX's collectives and lax.ppermute only.
A program may use at most 128 MiB of HBM per device.

```python
import math
import jax
import jax.numpy as jnp
from jax import lax

MODE_DEV = 32
MODES = 2048
NB = 256
BOX = 4
TBLK = 4
NT = 8
NOP = 4
LAT = 64
SP_DEV = 64
SPW = 256
NBLK = 2
ITEMS = 64
GROUPS = 32
CAP = 2
STOPW = 7
BCOL = 3072
N_MODE = 64
N_SPACE = 4


def draw_route(key, part):
    first, second, third = jax.random.split(key, 3)
    offsets = jax.random.permutation(first, N_MODE)[:GROUPS]
    local_order = jax.vmap(lambda sub: jax.random.permutation(sub, ITEMS))(jax.random.split(second, N_MODE))
    reader = jnp.arange(N_MODE)[:, None]
    slot = jnp.arange(ITEMS)[None, :]
    owner = (reader + offsets[slot // CAP]) % N_MODE
    value = owner * ITEMS + local_order[owner, jnp.broadcast_to(slot, owner.shape)]
    shuffle = jax.vmap(lambda sub: jax.random.permutation(sub, ITEMS))(jax.random.split(third, N_MODE))
    return jnp.take_along_axis(value, shuffle, axis=1).reshape(-1).astype(jnp.int32)


def plant(array, rng, smallest, high):
    longest = array.shape.index(max(array.shape))
    spots = []
    for shift in (0, 1):
        where = [jax.random.randint(jax.random.fold_in(rng, axis), (), 0, length) for axis, length in enumerate(array.shape)]
        where[longest] = (where[longest] + shift) % array.shape[longest]
        spots.append(tuple(where))
    return array.at[spots[0]].set(smallest).at[spots[1]].set(high)


def levels(key, shape, cuts, least, high):
    factor_of, own = 1.0, jax.random.fold_in(key, 6)
    for dim, shards_of in cuts:
        heights = jnp.exp(jax.random.uniform(jax.random.fold_in(own, dim), (shards_of,), jnp.float32, least / len(cuts), high / len(cuts)))
        factor_of = factor_of * jnp.repeat(heights, shape[dim] // shards_of).reshape([-1 if axis == dim else 1 for axis in range(len(shape))])
    return factor_of


def centred(rng, shape, scale, most, shards=(), held_as=jnp.bfloat16):
    factor_of = levels(rng, shape, shards, -0.22, 0.18) if shards else 1.0
    drawn = jax.random.normal(rng, shape, jnp.float32) * scale * factor_of
    return jnp.minimum(jnp.maximum(drawn, -most), most).astype(held_as)


def setup_inputs(seed: int = 0) -> dict:
    seeds = jax.random.split(jax.random.key(seed), 7)
    coefs = centred(seeds[0], (N_MODE * ITEMS, N_SPACE, 2, NB), 1.0, 6.0, ((0, 64), (1, 4)))
    counts = plant(jax.random.randint(seeds[1], (N_MODE * ITEMS, N_SPACE), 1, NB + 1), jax.random.fold_in(seeds[1], 1), 1, NB).astype(jnp.int32)
    route = draw_route(jax.random.fold_in(seeds[6], 71), 0)
    basis = centred(seeds[3], (N_SPACE * NBLK, 2, NB, BCOL), (NB * 4 * BOX * BOX) ** -0.5, 0.046875, ((0, 4),))
    momenta = plant(jax.random.randint(seeds[4], (NOP, 3), -3, 4), jax.random.fold_in(seeds[4], 1), -3, 3).astype(jnp.int32)
    gammas = plant(jax.random.randint(seeds[5], (NOP,), 0, 16), jax.random.fold_in(seeds[5], 1), 0, 15).astype(jnp.int32)
    return dict(coefs=coefs, counts=counts, route=route, basis=basis, momenta=momenta, gammas=gammas)


def expand(coefs, counts, route, basis):
    order = jnp.argsort(route).astype(jnp.int32)
    held = coefs[order]
    limit = counts[order]
    keep = jnp.arange(NB)[None, None, :] < limit[:, :, None]
    held = jnp.where(keep[:, :, None, :], held, jnp.zeros((), held.dtype))
    held = held.reshape(MODES, NBLK, N_SPACE, 2, NB).astype(jnp.float32)
    blocks = basis.reshape(N_SPACE, NBLK, 2, NB, BCOL).astype(jnp.float32)

    def product(coef_part, basis_part):
        return jnp.einsum("mbsn,sbnx->msbx", coef_part, basis_part)

    vec_re = product(held[:, :, :, 0], blocks[:, :, 0]) - product(held[:, :, :, 1], blocks[:, :, 1])
    vec_im = product(held[:, :, :, 0], blocks[:, :, 1]) + product(held[:, :, :, 1], blocks[:, :, 0])
    vectors = jnp.stack([vec_re, vec_im], axis=3).astype(jnp.bfloat16)
    vectors = vectors.reshape(MODES, N_SPACE, NBLK, 2, 4, 3, TBLK, SP_DEV)
    vectors = vectors.transpose(0, 2, 6, 3, 4, 5, 1, 7)
    return vectors.reshape(MODES, NT, 2, 4, 3, SPW)


def reference(coefs, counts, route, basis, momenta, gammas):
    vectors = expand(coefs, counts, route, basis)
    sites = jnp.arange(SPW)
    xs = sites % BOX
    ys = (sites // BOX) % BOX
    zs = sites // (BOX * BOX)
    inner = momenta[:, 0:1] * xs[None, :] + momenta[:, 1:2] * ys[None, :] + momenta[:, 2:3] * zs[None, :]
    turn = inner.astype(jnp.float32) * (2.0 * math.pi / LAT)
    cosine = jnp.cos(turn)[:, None, None, None, None, :]
    sine = jnp.sin(turn)[:, None, None, None, None, :]
    spins = jnp.arange(4)
    flip = gammas % 4
    bits = gammas // 4
    partner = jnp.bitwise_xor(spins[None, :], flip[:, None])
    common = jnp.bitwise_and(spins[None, :], bits[:, None])
    parity = (common % 2 + common // 2) % 2
    signs = (1 - 2 * parity).astype(jnp.float32)
    table = jnp.where(spins[None, None, :] == partner[:, :, None], signs[:, :, None], jnp.zeros((), jnp.float32))

    def owner_block(owner):
        resident = lax.dynamic_slice_in_dim(vectors, owner * MODE_DEV, MODE_DEV, 0).astype(jnp.float32)
        spun = jnp.einsum("osq,itpqcx->oitpscx", table, resident)
        w_re = (cosine * spun[:, :, :, 0] - sine * spun[:, :, :, 1]).astype(jnp.bfloat16)
        w_im = (sine * spun[:, :, :, 0] + cosine * spun[:, :, :, 1]).astype(jnp.bfloat16)
        w_re, w_im = lax.optimization_barrier((w_re, w_im))
        w_re = w_re.astype(jnp.float32)
        w_im = w_im.astype(jnp.float32)
        visiting = jnp.stack([lax.dynamic_slice_in_dim(vectors, ((owner - stop) % N_MODE) * MODE_DEV, MODE_DEV, 0) for stop in range(STOPW)]).astype(jnp.float32)
        v_re = visiting[:, :, :, 0]
        v_im = visiting[:, :, :, 1]
        form = "oitscx,vjtscx->tovji"
        real = jnp.einsum(form, w_re, v_re) + jnp.einsum(form, w_im, v_im)
        imag = jnp.einsum(form, w_re, v_im) - jnp.einsum(form, w_im, v_re)
        return jnp.stack([real, imag], axis=2)

    blocks = lax.map(owner_block, jnp.arange(N_MODE))
    return blocks.transpose(1, 2, 3, 4, 5, 0, 6).reshape(NT, NOP, 2, STOPW, MODE_DEV, MODES)
```

```python
import math

import jax
import jax.numpy as jnp
from jax import lax
from jax.experimental import pallas as pl
from jax.experimental.pallas import tpu as pltpu
from jax.sharding import PartitionSpec as P

LAT = 64
STOPW = 7
PLANES = 8
SPOTS = 8
ITEMS = 64
WIDTH = 256
MODES = 32
ROWS = STOPW * MODES
COLS = 768
OPS = 4
CAND = 128
Z_GROUPS = [[z * SPOTS + p for z in range(PLANES)] for p in range(SPOTS)]
P_GROUPS = [[z * SPOTS + p for p in range(SPOTS)] for z in range(PLANES)]
PAIRS = [(0, 1), (3, 4), (6, 7), (9, 10), (2, 5), (8, 11)]
BF16 = jnp.bfloat16
F32 = jnp.float32


def iota(shape, axis):
    return lax.broadcasted_iota(jnp.int32, shape, axis)


def pack_kernel(route_ref, coefs_ref, counts_ref, out_ref):
    me = lax.axis_index("mode")
    row = route_ref[pl.ds(me // 2, 1), :]
    row = jnp.where(me % 2 == 1, pltpu.roll(row, 64, 1), row)[:, :ITEMS]
    owner = lax.shift_right_logical(row, 6)
    i = iota((ITEMS, ITEMS), 0)
    j = iota((ITEMS, ITEMS), 1)
    owners = jnp.broadcast_to(owner, (ITEMS, ITEMS)).astype(F32)
    column = jnp.sum(jnp.where(i == j, owners, 0.0), axis=1, keepdims=True)
    earlier = jnp.where((owners == column) & (i < j), 1.0, 0.0)
    rank = jnp.max(earlier, axis=0, keepdims=True).astype(jnp.int32)
    target = owner * 2 + rank
    q = iota((PLANES * 32, ITEMS), 0)
    plane = (lax.shift_right_logical(q, 5) - (lax.shift_right_logical(q, 4) & 1)) & 7
    want = plane * 16 + (q & 15)
    outgoing = jnp.where(want == target, 1.0, 0.0).astype(BF16)
    keep = iota((ITEMS, WIDTH), 1) < counts_ref[...]
    for part in range(2):
        block = jnp.where(keep, coefs_ref[:, part, :].astype(F32), 0.0).astype(BF16)
        packed = jnp.dot(outgoing, block, preferred_element_type=F32)
        out_ref[:, part * WIDTH : (part + 1) * WIDTH] = packed.astype(BF16)


def forward_kernel(got_ref, out_ref, sorted_ref):
    n = PLANES * 32
    row = iota((n, n), 0)
    col = iota((n, n), 1)
    source = (lax.shift_right_logical(row, 1) & 7) * 32 + lax.shift_right_logical(row, 4) * 2 + (row & 1)
    order = jnp.where(col == source, 1.0, 0.0).astype(BF16)
    sorted_ref[...] = jnp.dot(order, got_ref[...], preferred_element_type=F32).astype(BF16)
    for spot in range(SPOTS):
        for stop in range(STOPW):
            block = ((spot - stop) % SPOTS) + (SPOTS if spot < stop else 0)
            out_ref[spot, stop * 16 : (stop + 1) * 16, :] = sorted_ref[block * 16 : (block + 1) * 16, :]


def tables_kernel(momenta_ref, gammas_ref, route_ref, placer_ref, table_ref):
    me = lax.axis_index("mode")
    route = route_ref[...]
    owner = lax.shift_right_logical(route, 6)
    key = iota(route.shape, 0) * ITEMS + (route & (ITEMS - 1))
    keyf = key.astype(F32)
    second = (iota((1, CAND), 1) & 1) == 1
    mode = iota((MODES, CAND), 0)
    for stop in range(STOPW):
        hit = owner == ((me - stop) & 63)
        low = jnp.min(jnp.where(hit, keyf, 8192.0), axis=0, keepdims=True)
        high = jnp.max(jnp.where(hit, keyf, -1.0), axis=0, keepdims=True)
        valid = jnp.where(second, high - low, 8000.0 - low) > 0.0
        item = jnp.where(second, high, low).astype(jnp.int32) & (ITEMS - 1)
        item = jnp.where(valid, item, -1)
        for block in range(2):
            placer_ref[block, stop] = jnp.where(mode * 2 + block == item, 1.0, 0.0).astype(BF16)
    place = lax.axis_index("space")
    lane = iota((1, 128), 1)
    site = place * 64 + (lane & 63)
    xs = site & 3
    ys = lax.shift_right_logical(site, 2) & 3
    zs = lax.shift_right_logical(site, 4)
    for op in range(OPS):
        inner = momenta_ref[op, 0] * xs + momenta_ref[op, 1] * ys + momenta_ref[op, 2] * zs
        turn = inner.astype(F32) * (2.0 * math.pi / LAT)
        cosine = jnp.cos(turn)
        sine = jnp.sin(turn)
        bits = lax.shift_right_logical(gammas_ref[op], 2)
        for group in range(6):
            spin = jnp.full((1, 128), group, jnp.int32) if group < 4 else 2 * (group - 4) + lax.shift_right_logical(lane, 6)
            common = spin & bits
            parity = (common ^ lax.shift_right_logical(common, 1)) & 1
            sign = (1 - 2 * parity).astype(F32)
            at = (op * 6 + group) * 2
            table_ref[at : at + 1, :] = cosine * sign
            table_ref[at + 1 : at + 2, :] = sine * sign


def sort_kernel(basis_ref, out_ref):
    low = iota((basis_ref.shape[1], 128), 1) < 64
    for group, (first, second) in enumerate(PAIRS):
        for pair in range(2):
            at = pair * 128
            a = basis_ref[0, :, first * 256 + at : first * 256 + at + 128].astype(F32)
            b = basis_ref[0, :, second * 256 + at : second * 256 + at + 128].astype(F32)
            lanes = slice(group * 128, (group + 1) * 128)
            out_ref[0, 2 * pair, :, lanes] = jnp.where(low, a, pltpu.roll(b, 64, 1)).astype(BF16)
            out_ref[0, 2 * pair + 1, :, lanes] = jnp.where(low, pltpu.roll(a, 64, 1), b).astype(BF16)


def window_kernel(where_ref, gammas_ref, got_ref, placer_ref, table_ref, basis_ref, out_ref, coef_ref, vec_ref, weight_ref):
    @pl.when(pl.program_id(0) == 0)
    def _():
        for stop in range(STOPW):
            rows = got_ref[:, stop * 16 : (stop + 1) * 16, :].reshape(CAND, 2 * WIDTH)
            coef = jnp.dot(placer_ref[0, stop], rows, preferred_element_type=F32)
            re = coef[:, :WIDTH]
            im = coef[:, WIDTH:]
            top = slice(stop * MODES, (stop + 1) * MODES)
            bottom = slice(ROWS + stop * MODES, ROWS + (stop + 1) * MODES)
            coef_ref[top, :WIDTH] = re.astype(BF16)
            coef_ref[top, WIDTH:] = (-im).astype(BF16)
            coef_ref[bottom, :WIDTH] = im.astype(BF16)
            coef_ref[bottom, WIDTH:] = re.astype(BF16)

    vec_ref[...] = jnp.dot(coef_ref[...], basis_ref[0, 0], preferred_element_type=F32).astype(BF16)
    for op in range(OPS):
        flip = gammas_ref[op] & 3
        for group in range(6):
            if group < 4:
                source = group ^ flip
            else:
                source = 4 + ((group - 4) ^ lax.shift_right_logical(flip, 1))
            lanes = pl.ds(pl.multiple_of(source * 128, 128), 128)
            re = vec_ref[0:MODES, lanes].astype(F32)
            im = vec_ref[ROWS : ROWS + MODES, lanes].astype(F32)
            if group >= 4:
                swap = (flip & 1) == 1
                re = jnp.where(swap, pltpu.roll(re, 64, 1), re)
                im = jnp.where(swap, pltpu.roll(im, 64, 1), im)
            at = (op * 6 + group) * 2
            cosine = table_ref[at : at + 1, :]
            sine = table_ref[at + 1 : at + 2, :]
            w_re = cosine * re - sine * im
            w_im = sine * re + cosine * im
            out_lanes = slice(group * 128, (group + 1) * 128)
            weight_ref[op * MODES : (op + 1) * MODES, out_lanes] = w_im.astype(BF16)
            weight_ref[128 + op * MODES : 128 + (op + 1) * MODES, out_lanes] = w_re.astype(BF16)
            weight_ref[256 + op * MODES : 256 + (op + 1) * MODES, out_lanes] = (-w_im).astype(BF16)
    contract = (((1,), (1,)), ((), ()))
    entries = lax.dot_general(vec_ref[:ROWS], weight_ref[128:], contract, preferred_element_type=F32)
    entries += lax.dot_general(vec_ref[ROWS:], weight_ref[:256], contract, preferred_element_type=F32)
    out_ref[0] = entries.astype(out_ref.dtype)


def total_kernel(own_ref, a_ref, b_ref, c_ref, out_ref):
    for t in range(2):
        total = own_ref[t] + a_ref[t].astype(F32) + b_ref[t].astype(F32) + c_ref[t].astype(F32)
        for r in range(2):
            for op in range(OPS):
                at = (r * OPS + op) * MODES
                out_ref[t, op, r] = total[:, at : at + MODES].reshape(STOPW, MODES, MODES)


VMEM = pl.BlockSpec(memory_space=pltpu.VMEM)
SMEM = pl.BlockSpec(memory_space=pltpu.SMEM)


def cost(flops, moved):
    return pl.CostEstimate(flops=flops, bytes_accessed=moved, transcendentals=0)


def window_part(where, gammas, got, placer, table, basis, dtype):
    spec = pltpu.PrefetchScalarGridSpec(
        num_scalar_prefetch=1,
        grid=(2,),
        in_specs=[
            SMEM,
            pl.BlockSpec((SPOTS, STOPW * 16, 2 * WIDTH), lambda i, w: (0, 0, 0)),
            pl.BlockSpec((1, STOPW, MODES, CAND), lambda i, w: (w[0] // 2, 0, 0, 0)),
            pl.BlockSpec((OPS * 12, 128), lambda i, w: (0, 0)),
            pl.BlockSpec((1, 1, 2 * WIDTH, COLS), lambda i, w: (w[0] // 2, 2 * (w[0] % 2) + i, 0, 0)),
        ],
        out_specs=pl.BlockSpec((1, ROWS, 256), lambda i, w: (i, 0, 0)),
        scratch_shapes=[
            pltpu.VMEM((2 * ROWS, 2 * WIDTH), BF16),
            pltpu.VMEM((2 * ROWS, COLS), BF16),
            pltpu.VMEM((384, COLS), BF16),
        ],
    )
    return pl.pallas_call(
        window_kernel,
        out_shape=jax.ShapeDtypeStruct((2, ROWS, 256), dtype),
        grid_spec=spec,
        compiler_params=pltpu.CompilerParams(vmem_limit_bytes=32 * 1024 * 1024),
        cost_estimate=cost(1_100_000_000, 3_000_000),
    )(where, gammas, got, placer, table, basis)


def per_device(coefs, counts, route, basis, momenta, gammas):
    place = lax.axis_index("space")
    packed = pl.pallas_call(
        pack_kernel,
        out_shape=jax.ShapeDtypeStruct((PLANES * 32, 2 * WIDTH), BF16),
        in_specs=[VMEM, VMEM, VMEM],
        out_specs=VMEM,
        cost_estimate=cost(20_000_000, 400_000),
    )(route.reshape(32, 128), coefs.reshape(ITEMS, 2, WIDTH), counts)
    first = lax.all_to_all(
        packed.reshape(PLANES, 32, 2 * WIDTH), "mode", 0, 0, tiled=True, axis_index_groups=Z_GROUPS
    )
    by_reader = route.reshape(PLANES, SPOTS, ITEMS).transpose(2, 1, 0).reshape(ITEMS, 64)
    by_reader = jnp.repeat(by_reader, 2, axis=1)
    placer, table = pl.pallas_call(
        tables_kernel,
        out_shape=(
            jax.ShapeDtypeStruct((2, STOPW, MODES, CAND), BF16),
            jax.ShapeDtypeStruct((OPS * 12, 128), F32),
        ),
        in_specs=[SMEM, SMEM, VMEM],
        out_specs=(VMEM, VMEM),
        cost_estimate=cost(2_000_000, 200_000),
    )(momenta, gammas, by_reader)
    sorted_basis = pl.pallas_call(
        sort_kernel,
        grid=(2, 4),
        out_shape=jax.ShapeDtypeStruct((2, 4, 2 * WIDTH, COLS), BF16),
        in_specs=[pl.BlockSpec((1, 128, 4 * COLS), lambda b, i: (b, i, 0))],
        out_specs=pl.BlockSpec((1, 4, 128, COLS), lambda b, i: (b, 0, i, 0)),
        cost_estimate=cost(10_000_000, 13_000_000),
    )(basis.reshape(2, 2 * WIDTH, 4 * COLS))
    onward = pl.pallas_call(
        forward_kernel,
        out_shape=jax.ShapeDtypeStruct((SPOTS, STOPW * 16, 2 * WIDTH), BF16),
        in_specs=[VMEM],
        out_specs=VMEM,
        scratch_shapes=[pltpu.VMEM((PLANES * 32, 2 * WIDTH), BF16)],
        cost_estimate=cost(70_000_000, 1_200_000),
    )(first.reshape(PLANES * 32, 2 * WIDTH))
    got = lax.all_to_all(onward, "mode", 0, 0, tiled=True, axis_index_groups=P_GROUPS)
    arrived = []
    for mask in (3, 2, 1):
        target = jnp.bitwise_xor(place, mask).reshape(1)
        part = window_part(target, gammas, got, placer, table, sorted_basis, BF16)
        arrived.append(lax.ppermute(part, "space", [(i, i ^ mask) for i in range(4)]))
    own = window_part(place.reshape(1), gammas, got, placer, table, sorted_basis, F32)
    return pl.pallas_call(
        total_kernel,
        out_shape=jax.ShapeDtypeStruct((2, OPS, 2, STOPW, MODES, MODES), F32),
        in_specs=[VMEM] * 4,
        out_specs=VMEM,
        cost_estimate=cost(1_000_000, 3_000_000),
    )(own, *arrived)


def solution(mesh):
    in_specs = (
        P("mode", "space", None, None),
        P("mode", "space"),
        P(),
        P("space", None, None, None),
        P(),
        P(),
    )
    out_specs = P("space", None, None, None, None, "mode")
    return jax.shard_map(
        per_device, mesh=mesh, in_specs=in_specs, out_specs=out_specs, check_vma=False
    )
```

```python
import functools
import math

import jax
import jax.numpy as jnp
from jax import lax
from jax.experimental import pallas as pl
from jax.experimental.pallas import tpu as pltpu
from jax.sharding import PartitionSpec as P

LAT = 64
STOPW = 7
PLANES = 8
SPOTS = 8
ITEMS = 64
WIDTH = 256
MODES = 32
ROWS = STOPW * MODES
COLS = 768
OPS = 4
CAND = 128
SPARE = 4
Z_GROUPS = [[z * SPOTS + p for z in range(PLANES)] for p in range(SPOTS)]
P_GROUPS = [[z * SPOTS + p for p in range(SPOTS)] for z in range(PLANES)]
PAIRS = [(0, 1), (3, 4), (6, 7), (9, 10), (2, 5), (8, 11)]
BF16 = jnp.bfloat16
F32 = jnp.float32


def iota(shape, axis):
    return lax.broadcasted_iota(jnp.int32, shape, axis)


def pack_kernel(route_ref, coefs_ref, counts_ref, out_ref):
    me = lax.axis_index("mode")
    row = route_ref[pl.ds(me // 2, 1), :]
    row = jnp.where(me % 2 == 1, pltpu.roll(row, 64, 1), row)[:, :ITEMS]
    owner = lax.shift_right_logical(row, 6)
    i = iota((ITEMS, ITEMS), 0)
    j = iota((ITEMS, ITEMS), 1)
    owners = jnp.broadcast_to(owner, (ITEMS, ITEMS)).astype(F32)
    column = jnp.sum(jnp.where(i == j, owners, 0.0), axis=1, keepdims=True)
    earlier = jnp.where((owners == column) & (i < j), 1.0, 0.0)
    rank = jnp.max(earlier, axis=0, keepdims=True).astype(jnp.int32)
    target = owner * 2 + rank
    q = iota((PLANES * 32, ITEMS), 0)
    plane = (lax.shift_right_logical(q, 5) - (lax.shift_right_logical(q, 4) & 1)) & 7
    want = plane * 16 + (q & 15)
    outgoing = jnp.where(want == target, 1.0, 0.0).astype(BF16)
    counts = jnp.broadcast_to(counts_ref[...], (ITEMS, ITEMS)).astype(F32)
    limit = jnp.sum(jnp.where(i == j, counts, 0.0), axis=1, keepdims=True).astype(jnp.int32)
    keep = iota((ITEMS, WIDTH), 1) < limit
    for part in range(2):
        block = jnp.where(keep, coefs_ref[:, part, :].astype(F32), 0.0).astype(BF16)
        packed = jnp.dot(outgoing, block, preferred_element_type=F32)
        out_ref[:, part * WIDTH : (part + 1) * WIDTH] = packed.astype(BF16)


def forward_kernel(got_ref, done_ref, out_ref, sorted_ref, sems):
    n = (SPOTS + STOPW - 1) * 16
    row = iota((n, PLANES * 32), 0)
    col = iota((n, PLANES * 32), 1)
    block = (SPOTS - 1 - lax.shift_right_logical(row, 4)) & 15
    source = (lax.shift_right_logical(row, 1) & 7) * 32 + block * 2 + (row & 1)
    order = jnp.where(col == source, 1.0, 0.0).astype(BF16)
    sorted_ref[...] = jnp.dot(order, got_ref[...], preferred_element_type=F32).astype(BF16)
    copies = []
    for spot in range(SPOTS):
        at = (SPOTS - 1 - spot) * 16
        copies.append(pltpu.make_async_copy(sorted_ref.at[at : at + STOPW * 16], out_ref.at[spot], sems.at[spot]))
    for copy in copies:
        copy.start()
    for copy in copies:
        copy.wait()


def tables_kernel(momenta_ref, gammas_ref, route_ref, placer_ref, table_ref):
    me = lax.axis_index("mode")
    route = route_ref[...]
    owner = lax.shift_right_logical(route, 6)
    key = iota(route.shape, 0) * ITEMS + (route & (ITEMS - 1))
    keyf = key.astype(F32)
    second = (iota((1, CAND), 1) & 1) == 1
    mode = iota((MODES, CAND), 0)
    for stop in range(STOPW):
        hit = owner == ((me - stop) & 63)
        low = jnp.min(jnp.where(hit, keyf, 8192.0), axis=0, keepdims=True)
        high = jnp.max(jnp.where(hit, keyf, -1.0), axis=0, keepdims=True)
        valid = jnp.where(second, high - low, 8000.0 - low) > 0.0
        item = jnp.where(second, high, low).astype(jnp.int32) & (ITEMS - 1)
        item = jnp.where(valid, item, -1)
        for block in range(2):
            placer_ref[stop, block * MODES : (block + 1) * MODES] = jnp.where(mode * 2 + block == item, 1.0, 0.0).astype(BF16)
    place = lax.axis_index("space")
    lane = iota((1, 128), 1)
    site = place * 64 + (lane & 63)
    xs = site & 3
    ys = lax.shift_right_logical(site, 2) & 3
    zs = lax.shift_right_logical(site, 4)
    for op in range(OPS):
        inner = momenta_ref[op, 0] * xs + momenta_ref[op, 1] * ys + momenta_ref[op, 2] * zs
        turn = inner.astype(F32) * (2.0 * math.pi / LAT)
        cosine = jnp.cos(turn)
        sine = jnp.sin(turn)
        bits = lax.shift_right_logical(gammas_ref[op], 2)
        for group in range(6):
            spin = jnp.full((1, 128), group, jnp.int32) if group < 4 else 2 * (group - 4) + lax.shift_right_logical(lane, 6)
            common = spin & bits
            parity = (common ^ lax.shift_right_logical(common, 1)) & 1
            sign = (1 - 2 * parity).astype(F32)
            at = (op * 6 + group) * 2
            table_ref[at : at + 1, :] = cosine * sign
            table_ref[at + 1 : at + 2, :] = sine * sign


def sort_kernel(basis_ref, out_ref, done_ref, slots_ref, sems):
    done_ref[...] = jnp.zeros(done_ref.shape, F32)
    step = 64
    low = iota((step, 128), 1) < 64

    def leave(chunk, slot):
        rows = pl.ds(pl.multiple_of(chunk * step, step), step)
        return pltpu.make_async_copy(slots_ref.at[slot], out_ref.at[0:2, :, rows, :], sems.at[slot])

    @pl.loop(0, 2 * WIDTH // step // 2)
    def _(turn):
        for slot in range(2):
            chunk = turn * 2 + slot

            @pl.when(turn > 0)
            def _():
                leave(chunk - 2, slot).wait()

            rows = pl.ds(pl.multiple_of(chunk * step, step), step)
            for block in range(2):
                for group, (first, second) in enumerate(PAIRS):
                    lanes = slice(group * 128, (group + 1) * 128)
                    for pair in range(2):
                        at = pair * 128
                        a = basis_ref[block, rows, first * 256 + at : first * 256 + at + 128].astype(F32)
                        b = basis_ref[block, rows, second * 256 + at : second * 256 + at + 128].astype(F32)
                        even = jnp.where(low, a, pltpu.roll(b, 64, 1))
                        odd = jnp.where(low, pltpu.roll(a, 64, 1), b)
                        slots_ref[slot, block, 2 * pair, :, lanes] = even.astype(BF16)
                        slots_ref[slot, block, 2 * pair + 1, :, lanes] = odd.astype(BF16)
            leave(chunk, slot).start()

    for slot in range(2):
        leave(2 * WIDTH // step - 2 + slot, slot).wait()


def fetch(sorted_ref, slab_ref, sems, mask):
    target = lax.axis_index("space") ^ mask
    block = lax.shift_right_logical(target, 1)
    first = 2 * (target & 1)
    return [
        pltpu.make_async_copy(sorted_ref.at[block, first + t], slab_ref.at[t], sems.at[t]) for t in range(2)
    ]


def place(got_ref, placer_ref, coef_ref):
    for stop in range(STOPW):
        rows = got_ref[:, stop * 16 : (stop + 1) * 16, :].reshape(CAND, 2 * WIDTH)
        coef = jnp.dot(placer_ref[stop], rows, preferred_element_type=F32)
        for block in range(2):
            re = coef[block * MODES : (block + 1) * MODES, :WIDTH]
            im = coef[block * MODES : (block + 1) * MODES, WIDTH:]
            top = slice(stop * MODES, (stop + 1) * MODES)
            bottom = slice(ROWS + stop * MODES, ROWS + (stop + 1) * MODES)
            coef_ref[block, top, :WIDTH] = re.astype(BF16)
            coef_ref[block, top, WIDTH:] = (-im).astype(BF16)
            coef_ref[block, bottom, :WIDTH] = im.astype(BF16)
            coef_ref[block, bottom, WIDTH:] = re.astype(BF16)


def first_kernel(mask, after, gammas_ref, table_ref, got_ref, placer_ref, sorted_ref, out_ref, coef_ref, next_ref, slab_ref, vec_ref, weight_ref, sems, next_sems):
    now = fetch(sorted_ref, slab_ref, sems, mask)
    later = fetch(sorted_ref, next_ref, next_sems, after)
    for copy in now + later:
        copy.start()
    place(got_ref, placer_ref, coef_ref)
    for copy in now:
        copy.wait()
    entries(mask, gammas_ref, table_ref, coef_ref, slab_ref, out_ref, vec_ref, weight_ref)
    for copy in later:
        copy.wait()


def middle_kernel(mask, after, gammas_ref, table_ref, coef_ref, slab_ref, sorted_ref, out_ref, next_ref, vec_ref, weight_ref, next_sems):
    later = fetch(sorted_ref, next_ref, next_sems, after)
    for copy in later:
        copy.start()
    entries(mask, gammas_ref, table_ref, coef_ref, slab_ref, out_ref, vec_ref, weight_ref)
    for copy in later:
        copy.wait()


def last_kernel(mask, after, gammas_ref, table_ref, coef_ref, slab_ref, sorted_ref, chip_ref, out_ref, own_ref, next_ref, vec_ref, weight_ref, next_sems):
    later = fetch(sorted_ref, next_ref, next_sems, after)
    for copy in later:
        copy.start()
    entries(mask, gammas_ref, table_ref, coef_ref, slab_ref, out_ref, vec_ref, weight_ref)
    for copy in later:
        copy.wait()
    entries(after, gammas_ref, table_ref, coef_ref, next_ref, own_ref, vec_ref, weight_ref)


def entries(mask, gammas_ref, table_ref, coef_ref, slab_ref, out_ref, vec_ref, weight_ref):
    block = lax.shift_right_logical(lax.axis_index("space") ^ mask, 1)
    for t in range(2):
        vec_ref[t] = jnp.dot(coef_ref[block], slab_ref[t], preferred_element_type=F32).astype(BF16)
    for t in range(2):
        for op in range(OPS):
            flip = gammas_ref[op] & 3
            for group in range(6):
                if group < 4:
                    source = group ^ flip
                else:
                    source = 4 + ((group - 4) ^ lax.shift_right_logical(flip, 1))
                lanes = pl.ds(pl.multiple_of(source * 128, 128), 128)
                re = vec_ref[t, 0:MODES, lanes].astype(F32)
                im = vec_ref[t, ROWS : ROWS + MODES, lanes].astype(F32)
                if group >= 4:
                    swap = (flip & 1) == 1
                    re = jnp.where(swap, pltpu.roll(re, 64, 1), re)
                    im = jnp.where(swap, pltpu.roll(im, 64, 1), im)
                at = (op * 6 + group) * 2
                cosine = table_ref[at : at + 1, :]
                sine = table_ref[at + 1 : at + 2, :]
                w_re = cosine * re - sine * im
                w_im = sine * re + cosine * im
                out_lanes = slice(group * 128, (group + 1) * 128)
                weight_ref[t, op * MODES : (op + 1) * MODES, out_lanes] = w_im.astype(BF16)
                weight_ref[t, 128 + op * MODES : 128 + (op + 1) * MODES, out_lanes] = w_re.astype(BF16)
                weight_ref[t, 256 + op * MODES : 256 + (op + 1) * MODES, out_lanes] = (-w_im).astype(BF16)
        contract = (((1,), (1,)), ((), ()))
        part = lax.dot_general(vec_ref[t, :ROWS], weight_ref[t, 128:], contract, preferred_element_type=F32)
        part += lax.dot_general(vec_ref[t, ROWS:], weight_ref[t, :256], contract, preferred_element_type=F32)
        out_ref[t] = part.astype(out_ref.dtype)


def pair_kernel(own_ref, other_ref, out_ref):
    out_ref[...] = (own_ref[...] + other_ref[...].astype(F32)).astype(BF16)


def total_kernel(own_ref, a_ref, b_ref, out_ref, total_ref, sems):
    copies = []
    for t in range(2):
        total = own_ref[t] + a_ref[t].astype(F32) + b_ref[t].astype(F32)
        for op in range(OPS):
            for r in range(2):
                at = (r * OPS + op) * MODES
                total_ref[t, op, r] = total[:, at : at + MODES].reshape(STOPW, MODES, MODES)
            copy = pltpu.make_async_copy(total_ref.at[t, op], out_ref.at[t, op], sems.at[t, op])
            copy.start()
            copies.append(copy)
    for copy in copies:
        copy.wait()


VMEM = pl.BlockSpec(memory_space=pltpu.VMEM)
SMEM = pl.BlockSpec(memory_space=pltpu.SMEM)
HBM = pl.BlockSpec(memory_space=pltpu.HBM)
DMA = pltpu.SemaphoreType.DMA


def kernel_call(kernel, out_shape, in_specs, flops, moved, scratch=(), limit=8, out_specs=None):
    many = isinstance(out_shape, tuple)
    return pl.pallas_call(
        kernel,
        out_shape=out_shape,
        in_specs=in_specs,
        out_specs=out_specs or ((VMEM,) * len(out_shape) if many else VMEM),
        scratch_shapes=list(scratch),
        compiler_params=pltpu.CompilerParams(vmem_limit_bytes=limit * 1024 * 1024),
        cost_estimate=pl.CostEstimate(flops=flops, bytes_accessed=moved, transcendentals=0),
    )


def shape(dims, dtype=BF16):
    return jax.ShapeDtypeStruct(dims, dtype)


def per_device(coefs, counts, route, basis, momenta, gammas):
    packed = kernel_call(
        pack_kernel, shape((PLANES * 32, 2 * WIDTH)), [VMEM] * 3, 20_000_000, 400_000
    )(route.reshape(32, 128), coefs.reshape(ITEMS, 2, WIDTH), counts.reshape(1, ITEMS))
    first = lax.all_to_all(
        packed.reshape(PLANES, 32, 2 * WIDTH), "mode", 0, 0, tiled=True, axis_index_groups=Z_GROUPS
    )
    by_reader = route.reshape(PLANES, SPOTS, ITEMS).transpose(2, 1, 0).reshape(ITEMS, 64)
    by_reader = jnp.repeat(by_reader, 2, axis=1)
    placer, table = kernel_call(
        tables_kernel,
        (shape((STOPW, ITEMS, CAND)), shape((OPS * 12, 128), F32)),
        [SMEM, SMEM, VMEM],
        2_000_000,
        200_000,
    )(momenta, gammas, by_reader)
    sorted_basis, done = kernel_call(
        sort_kernel,
        (shape((SPARE * 2, 4, 2 * WIDTH, COLS)), shape((8, 128), F32)),
        [VMEM],
        10_000_000,
        13_000_000,
        [pltpu.VMEM((2, 2, 4, 64, COLS), BF16), DMA((2,))],
        limit=44,
        out_specs=(HBM, VMEM),
    )(basis.reshape(2, 2 * WIDTH, 4 * COLS))
    onward = kernel_call(
        forward_kernel,
        shape((SPOTS, STOPW * 16, 2 * WIDTH)),
        [VMEM, VMEM],
        70_000_000,
        1_200_000,
        [pltpu.VMEM(((SPOTS + STOPW - 1) * 16, 2 * WIDTH), BF16), DMA((SPOTS,))],
        out_specs=HBM,
    )(first.reshape(PLANES * 32, 2 * WIDTH), done)
    got = lax.all_to_all(onward, "mode", 0, 0, tiled=True, axis_index_groups=P_GROUPS)
    part_shape = shape((2, ROWS, 256))
    coef_shape = shape((2, 2 * ROWS, 2 * WIDTH))
    slab_shape = shape((2, 2 * WIDTH, COLS))
    work = [pltpu.VMEM((2, 2 * ROWS, COLS), BF16), pltpu.VMEM((2, 384, COLS), BF16)]
    part_3, coef, slab = kernel_call(
        functools.partial(first_kernel, 3, 2),
        (part_shape, coef_shape, slab_shape),
        [SMEM, VMEM, VMEM, VMEM, HBM],
        1_100_000_000,
        5_000_000,
        [pltpu.VMEM((2, 2 * WIDTH, COLS), BF16)] + work + [DMA((2,)), DMA((2,))],
        limit=44,
    )(gammas, table, got, placer, sorted_basis)
    def between(pair, part):
        return lax.ppermute(part, "space", [(i, i ^ pair) for i in range(4)])

    part_2, slab = kernel_call(
        functools.partial(middle_kernel, 2, 1),
        (shape((2, ROWS, 256), F32), slab_shape),
        [SMEM, VMEM, VMEM, VMEM, HBM],
        1_100_000_000,
        4_000_000,
        work + [DMA((2,))],
        limit=44,
    )(gammas, table, coef, slab, sorted_basis)
    chip = kernel_call(pair_kernel, part_shape, [VMEM] * 2, 200_000, 900_000)(part_2, between(1, part_3))
    far = between(2, chip)
    part_1, own = kernel_call(
        functools.partial(last_kernel, 1, 0),
        (part_shape, shape((2, ROWS, 256), F32)),
        [SMEM, VMEM, VMEM, VMEM, HBM, VMEM],
        2_200_000_000,
        4_000_000,
        [pltpu.VMEM((2, 2 * WIDTH, COLS), BF16)] + work + [DMA((2,))],
        limit=44,
    )(gammas, table, coef, slab, sorted_basis, chip)
    part_1, far = lax.optimization_barrier((part_1, far))
    near = between(1, part_1)
    return kernel_call(
        total_kernel,
        shape((2, OPS, 2, STOPW, MODES, MODES), F32),
        [VMEM] * 3,
        1_000_000,
        3_000_000,
        [pltpu.VMEM((2, OPS, 2, STOPW, MODES, MODES), F32), DMA((2, OPS))],
        out_specs=HBM,
    )(own, far, near)


def solution(mesh):
    in_specs = (
        P("mode", "space", None, None),
        P("mode", "space"),
        P(),
        P("space", None, None, None),
        P(),
        P(),
    )
    out_specs = P("space", None, None, None, None, "mode")
    return jax.shard_map(
        per_device, mesh=mesh, in_specs=in_specs, out_specs=out_specs, check_vma=False
    )
```

```python
import functools
import math

import jax
import jax.numpy as jnp
from jax import lax
from jax.experimental import pallas as pl
from jax.experimental.pallas import tpu as pltpu
from jax.sharding import PartitionSpec as P

LAT = 64
STOPW = 7
PLANES = 8
SPOTS = 8
ITEMS = 64
WIDTH = 256
MODES = 32
ROWS = STOPW * MODES
COLS = 768
OPS = 4
CAND = 128
SPARE = 4
Z_GROUPS = [[z * SPOTS + p for z in range(PLANES)] for p in range(SPOTS)]
P_GROUPS = [[z * SPOTS + p for p in range(SPOTS)] for z in range(PLANES)]
PAIRS = [(0, 1), (3, 4), (6, 7), (9, 10), (2, 5), (8, 11)]
BF16 = jnp.bfloat16
F32 = jnp.float32


def iota(shape, axis):
    return lax.broadcasted_iota(jnp.int32, shape, axis)


def pack_kernel(route_ref, coefs_ref, counts_ref, out_ref):
    me = lax.axis_index("mode")
    row = route_ref[pl.ds(me // 2, 1), :]
    row = jnp.where(me % 2 == 1, pltpu.roll(row, 64, 1), row)[:, :ITEMS]
    owner = lax.shift_right_logical(row, 6)
    i = iota((ITEMS, ITEMS), 0)
    j = iota((ITEMS, ITEMS), 1)
    owners = jnp.broadcast_to(owner, (ITEMS, ITEMS)).astype(F32)
    column = jnp.sum(jnp.where(i == j, owners, 0.0), axis=1, keepdims=True)
    earlier = jnp.where((owners == column) & (i < j), 1.0, 0.0)
    rank = jnp.max(earlier, axis=0, keepdims=True).astype(jnp.int32)
    target = owner * 2 + rank
    q = iota((PLANES * 32, ITEMS), 0)
    plane = (lax.shift_right_logical(q, 5) - (lax.shift_right_logical(q, 4) & 1)) & 7
    want = plane * 16 + (q & 15)
    outgoing = jnp.where(want == target, 1.0, 0.0).astype(BF16)
    counts = jnp.broadcast_to(counts_ref[...], (ITEMS, ITEMS)).astype(F32)
    limit = jnp.sum(jnp.where(i == j, counts, 0.0), axis=1, keepdims=True).astype(jnp.int32)
    keep = iota((ITEMS, WIDTH), 1) < limit
    for part in range(2):
        block = jnp.where(keep, coefs_ref[:, part, :].astype(F32), 0.0).astype(BF16)
        packed = jnp.dot(outgoing, block, preferred_element_type=F32)
        out_ref[:, part * WIDTH : (part + 1) * WIDTH] = packed.astype(BF16)


def forward_kernel(got_ref, done_ref, table_ref, out_ref, sorted_ref, sems):
    n = (SPOTS + STOPW - 1) * 16
    row = iota((n, PLANES * 32), 0)
    col = iota((n, PLANES * 32), 1)
    block = (SPOTS - 1 - lax.shift_right_logical(row, 4)) & 15
    source = (lax.shift_right_logical(row, 1) & 7) * 32 + block * 2 + (row & 1)
    order = jnp.where(col == source, 1.0, 0.0).astype(BF16)
    sorted_ref[...] = jnp.dot(order, got_ref[...], preferred_element_type=F32).astype(BF16)
    copies = []
    for spot in range(SPOTS):
        at = (SPOTS - 1 - spot) * 16
        copies.append(pltpu.make_async_copy(sorted_ref.at[at : at + STOPW * 16], out_ref.at[spot], sems.at[spot]))
    for copy in copies:
        copy.start()
    for copy in copies:
        copy.wait()


def tables_kernel(momenta_ref, gammas_ref, route_ref, placer_ref, table_ref):
    me = lax.axis_index("mode")
    route = route_ref[...]
    owner = lax.shift_right_logical(route, 6)
    key = iota(route.shape, 0) * ITEMS + (route & (ITEMS - 1))
    keyf = key.astype(F32)
    second = (iota((1, CAND), 1) & 1) == 1
    mode = iota((MODES, CAND), 0)
    for stop in range(STOPW):
        hit = owner == ((me - stop) & 63)
        low = jnp.min(jnp.where(hit, keyf, 8192.0), axis=0, keepdims=True)
        high = jnp.max(jnp.where(hit, keyf, -1.0), axis=0, keepdims=True)
        valid = jnp.where(second, high - low, 8000.0 - low) > 0.0
        item = jnp.where(second, high, low).astype(jnp.int32) & (ITEMS - 1)
        item = jnp.where(valid, item, -1)
        for block in range(2):
            placer_ref[block, stop] = jnp.where(mode * 2 + block == item, 1.0, 0.0).astype(BF16)
    place = lax.axis_index("space")
    lane = iota((1, 128), 1)
    site = place * 64 + (lane & 63)
    xs = site & 3
    ys = lax.shift_right_logical(site, 2) & 3
    zs = lax.shift_right_logical(site, 4)
    for op in range(OPS):
        inner = momenta_ref[op, 0] * xs + momenta_ref[op, 1] * ys + momenta_ref[op, 2] * zs
        turn = inner.astype(F32) * (2.0 * math.pi / LAT)
        cosine = jnp.cos(turn)
        sine = jnp.sin(turn)
        bits = lax.shift_right_logical(gammas_ref[op], 2)
        for group in range(6):
            spin = jnp.full((1, 128), group, jnp.int32) if group < 4 else 2 * (group - 4) + lax.shift_right_logical(lane, 6)
            common = spin & bits
            parity = (common ^ lax.shift_right_logical(common, 1)) & 1
            sign = (1 - 2 * parity).astype(F32)
            at = (op * 6 + group) * 2
            table_ref[at : at + 1, :] = cosine * sign
            table_ref[at + 1 : at + 2, :] = sine * sign


def sort_kernel(basis_ref, out_ref, done_ref, reads_ref, slots_ref, in_sems, sems):
    done_ref[...] = jnp.zeros(done_ref.shape, F32)
    step = 64
    chunks = 2 * WIDTH // step
    low = iota((step, 128), 1) < 64

    def take(chunk, slot):
        rows = pl.ds(pl.multiple_of(chunk * step, step), step)
        return pltpu.make_async_copy(basis_ref.at[:, rows, :], reads_ref.at[slot], in_sems.at[slot])

    def leave(chunk, slot):
        rows = pl.ds(pl.multiple_of(chunk * step, step), step)
        return pltpu.make_async_copy(slots_ref.at[slot], out_ref.at[0:2, :, rows, :], sems.at[slot])

    for slot in range(2):
        take(slot, slot).start()

    @pl.loop(0, chunks // 2)
    def _(turn):
        for slot in range(2):
            chunk = turn * 2 + slot
            take(chunk, slot).wait()

            @pl.when(turn > 0)
            def _():
                leave(chunk - 2, slot).wait()

            for block in range(2):
                for group, (first, second) in enumerate(PAIRS):
                    lanes = slice(group * 128, (group + 1) * 128)
                    for pair in range(2):
                        at = pair * 128
                        a = reads_ref[slot, block, :, first * 256 + at : first * 256 + at + 128]
                        b = reads_ref[slot, block, :, second * 256 + at : second * 256 + at + 128]
                        slots_ref[slot, block, 2 * pair, :, lanes] = jnp.where(low, a, pltpu.roll(b, 64, 1))
                        slots_ref[slot, block, 2 * pair + 1, :, lanes] = jnp.where(low, pltpu.roll(a, 64, 1), b)
            leave(chunk, slot).start()

            @pl.when(turn < chunks // 2 - 1)
            def _():
                take(chunk + 2, slot).start()

    for slot in range(2):
        leave(chunks - 2 + slot, slot).wait()


def block_of(mask):
    return lax.shift_right_logical(lax.axis_index("space") ^ mask, 1)


def fetch(sorted_ref, slab_ref, sem, mask, t):
    target = lax.axis_index("space") ^ mask
    return pltpu.make_async_copy(sorted_ref.at[block_of(mask), 2 * (target & 1) + t], slab_ref, sem)


def place(block, got_ref, placer_ref, coef_ref):
    for stop in range(STOPW):
        rows = got_ref[:, stop * 16 : (stop + 1) * 16, :].reshape(CAND, 2 * WIDTH)
        coef = jnp.dot(placer_ref[block, stop], rows, preferred_element_type=F32)
        re = coef[:, :WIDTH]
        im = coef[:, WIDTH:]
        top = slice(stop * MODES, (stop + 1) * MODES)
        bottom = slice(ROWS + stop * MODES, ROWS + (stop + 1) * MODES)
        coef_ref[top, :WIDTH] = re.astype(BF16)
        coef_ref[top, WIDTH:] = (-im).astype(BF16)
        coef_ref[bottom, :WIDTH] = im.astype(BF16)
        coef_ref[bottom, WIDTH:] = re.astype(BF16)


def entries(gammas_ref, table_ref, coef_ref, slab_ref, vec_ref, weight_ref):
    vec = jnp.dot(coef_ref[...], slab_ref[...], preferred_element_type=F32).astype(BF16)
    vec_ref[:, :COLS] = vec[:ROWS]
    vec_ref[:, COLS:] = vec[ROWS:]
    for op in range(OPS):
        flip = gammas_ref[op] & 3
        for group in range(6):
            if group < 4:
                source = group ^ flip
            else:
                source = 4 + ((group - 4) ^ lax.shift_right_logical(flip, 1))
            start = pl.multiple_of(source * 128, 128)
            re = vec_ref[0:MODES, pl.ds(start, 128)].astype(F32)
            im = vec_ref[0:MODES, pl.ds(start + COLS, 128)].astype(F32)
            if group >= 4:
                swap = (flip & 1) == 1
                re = jnp.where(swap, pltpu.roll(re, 64, 1), re)
                im = jnp.where(swap, pltpu.roll(im, 64, 1), im)
            at = (op * 6 + group) * 2
            cosine = table_ref[at : at + 1, :]
            sine = table_ref[at + 1 : at + 2, :]
            w_re = cosine * re - sine * im
            w_im = sine * re + cosine * im
            real = slice(op * MODES, (op + 1) * MODES)
            imag = slice(128 + op * MODES, 128 + (op + 1) * MODES)
            left = slice(group * 128, (group + 1) * 128)
            right = slice(COLS + group * 128, COLS + (group + 1) * 128)
            weight_ref[real, left] = w_re.astype(BF16)
            weight_ref[real, right] = w_im.astype(BF16)
            weight_ref[imag, left] = (-w_im).astype(BF16)
            weight_ref[imag, right] = w_re.astype(BF16)
    return lax.dot_general(vec_ref[...], weight_ref[...], (((1,), (1,)), ((), ())), preferred_element_type=F32)


def first_kernel(now, after, gammas_ref, table_ref, got_ref, placer_ref, sorted_ref, out_ref, coef_ref, next_ref, slab_ref, vec_ref, weight_ref, sems):
    slab = fetch(sorted_ref, slab_ref, sems.at[0], *now)
    later = fetch(sorted_ref, next_ref, sems.at[1], *after)
    slab.start()
    later.start()
    place(block_of(now[0]), got_ref, placer_ref, coef_ref)
    slab.wait()
    out_ref[...] = entries(gammas_ref, table_ref, coef_ref, slab_ref, vec_ref, weight_ref).astype(BF16)
    later.wait()


def middle_kernel(after, gammas_ref, table_ref, coef_ref, slab_ref, sorted_ref, *rest):
    out_ref, next_ref, vec_ref, weight_ref, sem = rest[-5:]
    later = fetch(sorted_ref, next_ref, sem, *after)
    later.start()
    total = entries(gammas_ref, table_ref, coef_ref, slab_ref, vec_ref, weight_ref)
    if len(rest) > 5:
        total = total + rest[0][...].astype(F32)
    out_ref[...] = total.astype(BF16)
    later.wait()


def last_kernel(steps, gammas_ref, table_ref, got_ref, placer_ref, slab_ref, sorted_ref, before_ref, part_a_ref, part_b_ref, own_ref, coef_ref, slabs_ref, vec_ref, weight_ref, sems):
    place(block_of(0), got_ref, placer_ref, coef_ref)
    copies = [None] + [
        fetch(sorted_ref, slabs_ref.at[n % 2], sems.at[n % 2], *step) for n, step in enumerate(steps) if n > 0
    ]
    copies[1].start()
    for n, (mask, t) in enumerate(steps):
        if n > 0:
            copies[n].wait()
        if 0 < n < len(steps) - 1:
            copies[n + 1].start()
        slab = slab_ref if n == 0 else slabs_ref.at[n % 2]
        total = entries(gammas_ref, table_ref, coef_ref, slab, vec_ref.at[n % 2], weight_ref.at[n % 2])
        if mask == 1:
            (part_a_ref, part_b_ref)[t][...] = total.astype(BF16)
        else:
            own_ref[t] = total


def total_kernel(own_ref, near_a_ref, near_b_ref, far_a_ref, far_b_ref, out_ref, total_ref, sems):
    copies = []
    for t, (near_ref, far_ref) in enumerate(((near_a_ref, far_a_ref), (near_b_ref, far_b_ref))):
        total = own_ref[t] + near_ref[...].astype(F32) + far_ref[...].astype(F32)
        for op in range(OPS):
            for r in range(2):
                at = (r * OPS + op) * MODES
                total_ref[t, op, r] = total[:, at : at + MODES].reshape(STOPW, MODES, MODES)
            copy = pltpu.make_async_copy(total_ref.at[t, op], out_ref.at[t, op], sems.at[t, op])
            copy.start()
            copies.append(copy)
    for copy in copies:
        copy.wait()


VMEM = pl.BlockSpec(memory_space=pltpu.VMEM)
SMEM = pl.BlockSpec(memory_space=pltpu.SMEM)
HBM = pl.BlockSpec(memory_space=pltpu.HBM)
DMA = pltpu.SemaphoreType.DMA


def kernel_call(kernel, out_shape, in_specs, flops, moved, scratch=(), limit=8, out_specs=None):
    many = isinstance(out_shape, tuple)
    return pl.pallas_call(
        kernel,
        out_shape=out_shape,
        in_specs=in_specs,
        out_specs=out_specs or ((VMEM,) * len(out_shape) if many else VMEM),
        scratch_shapes=list(scratch),
        compiler_params=pltpu.CompilerParams(vmem_limit_bytes=limit * 1024 * 1024),
        cost_estimate=pl.CostEstimate(flops=flops, bytes_accessed=moved, transcendentals=0),
    )


def shape(dims, dtype=BF16):
    return jax.ShapeDtypeStruct(dims, dtype)


def per_device(coefs, counts, route, basis, momenta, gammas):
    packed = kernel_call(
        pack_kernel, shape((PLANES * 32, 2 * WIDTH)), [VMEM] * 3, 20_000_000, 400_000, limit=60
    )(route.reshape(32, 128), coefs.reshape(ITEMS, 2, WIDTH), counts.reshape(1, ITEMS))
    first = lax.all_to_all(
        packed.reshape(PLANES, 32, 2 * WIDTH), "mode", 0, 0, tiled=True, axis_index_groups=Z_GROUPS
    )
    by_reader = route.reshape(PLANES, SPOTS, ITEMS).transpose(2, 1, 0).reshape(ITEMS, 64)
    by_reader = jnp.repeat(by_reader, 2, axis=1)
    placer, table = kernel_call(
        tables_kernel,
        (shape((2, STOPW, MODES, CAND)), shape((OPS * 12, 128), F32)),
        [SMEM, SMEM, VMEM],
        2_000_000,
        200_000,
    )(momenta, gammas, by_reader)
    sorted_basis, done = kernel_call(
        sort_kernel,
        (shape((SPARE * 2, 4, 2 * WIDTH, COLS)), shape((8, 128), F32)),
        [HBM],
        10_000_000,
        13_000_000,
        [
            pltpu.VMEM((2, 2, 64, 4 * COLS), BF16),
            pltpu.VMEM((2, 2, 4, 64, COLS), BF16),
            DMA((2,)),
            DMA((2,)),
        ],
        limit=60,
        out_specs=(HBM, VMEM),
    )(basis.reshape(2, 2 * WIDTH, 4 * COLS))
    onward = kernel_call(
        forward_kernel,
        shape((SPOTS, STOPW * 16, 2 * WIDTH)),
        [VMEM, VMEM, VMEM],
        70_000_000,
        1_200_000,
        [pltpu.VMEM(((SPOTS + STOPW - 1) * 16, 2 * WIDTH), BF16), DMA((SPOTS,))],
        out_specs=HBM,
    )(first.reshape(PLANES * 32, 2 * WIDTH), done, table)
    got = lax.all_to_all(onward, "mode", 0, 0, tiled=True, axis_index_groups=P_GROUPS)
    part_shape = shape((ROWS, 256))
    slab_shape = shape((2 * WIDTH, COLS))
    vec_shape = (ROWS, 2 * COLS)
    weight_shape = (256, 2 * COLS)
    work = [pltpu.VMEM(vec_shape, BF16), pltpu.VMEM(weight_shape, BF16)]

    def between(pair, part):
        return lax.ppermute(part, "space", [(i, i ^ pair) for i in range(4)])

    def middle(slab, after, *extra):
        return kernel_call(
            functools.partial(middle_kernel, after),
            (part_shape, slab_shape),
            [SMEM, VMEM, VMEM, VMEM, HBM] + [VMEM] * len(extra),
            550_000_000,
            2_000_000,
            work + [DMA],
            limit=44,
        )(gammas, table, coef, slab, sorted_basis, *extra)

    other_a, coef, slab = kernel_call(
        functools.partial(first_kernel, (3, 0), (3, 1)),
        (part_shape, shape((2 * ROWS, 2 * WIDTH)), slab_shape),
        [SMEM, VMEM, VMEM, VMEM, HBM],
        600_000_000,
        3_000_000,
        [pltpu.VMEM((2 * WIDTH, COLS), BF16)] + work + [DMA((2,))],
        limit=44,
    )(gammas, table, got, placer, sorted_basis)
    other_b, slab = middle(slab, (2, 0))
    chip_a, slab = middle(slab, (2, 1), between(1, other_a))
    far_a = between(2, chip_a)
    chip_b, slab = middle(slab, (1, 0), between(1, other_b))
    far_b = between(2, chip_b)
    part_a, part_b, own = kernel_call(
        functools.partial(last_kernel, ((1, 0), (1, 1), (0, 0), (0, 1))),
        (part_shape, part_shape, shape((2, ROWS, 256), F32)),
        [SMEM, VMEM, VMEM, VMEM, VMEM, HBM, VMEM],
        2_200_000_000,
        6_000_000,
        [
            pltpu.VMEM((2 * ROWS, 2 * WIDTH), BF16),
            pltpu.VMEM((2, 2 * WIDTH, COLS), BF16),
            pltpu.VMEM((2, *vec_shape), BF16),
            pltpu.VMEM((2, *weight_shape), BF16),
            DMA((2,)),
        ],
        limit=44,
    )(gammas, table, got, placer, slab, sorted_basis, chip_b)
    part_a, part_b, far_a = lax.optimization_barrier((part_a, part_b, far_a))
    near_a = between(1, part_a)
    near_b = between(1, part_b)
    return kernel_call(
        total_kernel,
        shape((2, OPS, 2, STOPW, MODES, MODES), F32),
        [VMEM] * 5,
        1_000_000,
        3_000_000,
        [pltpu.VMEM((2, OPS, 2, STOPW, MODES, MODES), F32), DMA((2, OPS))],
        out_specs=HBM,
    )(own, near_a, near_b, far_a, far_b)


def solution(mesh):
    in_specs = (
        P("mode", "space", None, None),
        P("mode", "space"),
        P(),
        P("space", None, None, None),
        P(),
        P(),
    )
    out_specs = P("space", None, None, None, None, "mode")
    return jax.shard_map(
        per_device, mesh=mesh, in_specs=in_specs, out_specs=out_specs, check_vma=False
    )
```

```python
import functools
import math

import jax
import jax.numpy as jnp
from jax import lax
from jax.experimental import pallas as pl
from jax.experimental.pallas import tpu as pltpu
from jax.sharding import PartitionSpec as P

LAT = 64
STOPW = 7
PLANES = 8
SPOTS = 8
ITEMS = 64
WIDTH = 256
MODES = 32
ROWS = STOPW * MODES
COLS = 768
OPS = 4
CAND = 128
Z_GROUPS = [[z * SPOTS + p for z in range(PLANES)] for p in range(SPOTS)]
P_GROUPS = [[z * SPOTS + p for p in range(SPOTS)] for z in range(PLANES)]
PAIRS = [(0, 1), (3, 4), (6, 7), (9, 10), (2, 5), (8, 11)]
BF16 = jnp.bfloat16
F32 = jnp.float32


def iota(shape, axis):
    return lax.broadcasted_iota(jnp.int32, shape, axis)


def pack_kernel(route_ref, coefs_ref, counts_ref, out_ref):
    me = lax.axis_index("mode")
    row = route_ref[pl.ds(me // 2, 1), :]
    row = jnp.where(me % 2 == 1, pltpu.roll(row, 64, 1), row)[:, :ITEMS]
    owner = lax.shift_right_logical(row, 6)
    i = iota((ITEMS, ITEMS), 0)
    j = iota((ITEMS, ITEMS), 1)
    owners = jnp.broadcast_to(owner, (ITEMS, ITEMS)).astype(F32)
    column = jnp.sum(jnp.where(i == j, owners, 0.0), axis=1, keepdims=True)
    earlier = jnp.where((owners == column) & (i < j), 1.0, 0.0)
    rank = jnp.max(earlier, axis=0, keepdims=True).astype(jnp.int32)
    target = owner * 2 + rank
    q = iota((PLANES * 32, ITEMS), 0)
    plane = (lax.shift_right_logical(q, 5) - (lax.shift_right_logical(q, 4) & 1)) & 7
    want = plane * 16 + (q & 15)
    outgoing = jnp.where(want == target, 1.0, 0.0).astype(BF16)
    counts = jnp.broadcast_to(counts_ref[...], (ITEMS, ITEMS)).astype(F32)
    limit = jnp.sum(jnp.where(i == j, counts, 0.0), axis=1, keepdims=True).astype(jnp.int32)
    keep = iota((ITEMS, WIDTH), 1) < limit
    for part in range(2):
        block = jnp.where(keep, coefs_ref[:, part, :].astype(F32), 0.0).astype(BF16)
        packed = jnp.dot(outgoing, block, preferred_element_type=F32)
        out_ref[:, part * WIDTH : (part + 1) * WIDTH] = packed.astype(BF16)


def forward_kernel(got_ref, done_ref, table_ref, out_ref, sorted_ref, sems):
    n = (SPOTS + STOPW - 1) * 16
    row = iota((n, PLANES * 32), 0)
    col = iota((n, PLANES * 32), 1)
    block = (SPOTS - 1 - lax.shift_right_logical(row, 4)) & 15
    source = (lax.shift_right_logical(row, 1) & 7) * 32 + block * 2 + (row & 1)
    order = jnp.where(col == source, 1.0, 0.0).astype(BF16)
    sorted_ref[...] = jnp.dot(order, got_ref[...], preferred_element_type=F32).astype(BF16)
    copies = []
    for spot in range(SPOTS):
        at = (SPOTS - 1 - spot) * 16
        copies.append(pltpu.make_async_copy(sorted_ref.at[at : at + STOPW * 16], out_ref.at[spot], sems.at[spot]))
    for copy in copies:
        copy.start()
    for copy in copies:
        copy.wait()


def tables_kernel(momenta_ref, gammas_ref, route_ref, placer_ref, table_ref):
    me = lax.axis_index("mode")
    route = route_ref[...]
    owner = lax.shift_right_logical(route, 6)
    key = iota(route.shape, 0) * ITEMS + (route & (ITEMS - 1))
    keyf = key.astype(F32)
    second = (iota((1, CAND), 1) & 1) == 1
    mode = iota((MODES, CAND), 0)
    for stop in range(STOPW):
        hit = owner == ((me - stop) & 63)
        low = jnp.min(jnp.where(hit, keyf, 8192.0), axis=0, keepdims=True)
        high = jnp.max(jnp.where(hit, keyf, -1.0), axis=0, keepdims=True)
        valid = jnp.where(second, high - low, 8000.0 - low) > 0.0
        item = jnp.where(second, high, low).astype(jnp.int32) & (ITEMS - 1)
        item = jnp.where(valid, item, -1)
        for block in range(2):
            placer_ref[block, stop] = jnp.where(mode * 2 + block == item, 1.0, 0.0).astype(BF16)
    place = lax.axis_index("space")
    lane = iota((1, 128), 1)
    site = place * 64 + (lane & 63)
    xs = site & 3
    ys = lax.shift_right_logical(site, 2) & 3
    zs = lax.shift_right_logical(site, 4)
    for op in range(OPS):
        inner = momenta_ref[op, 0] * xs + momenta_ref[op, 1] * ys + momenta_ref[op, 2] * zs
        turn = inner.astype(F32) * (2.0 * math.pi / LAT)
        cosine = jnp.cos(turn)
        sine = jnp.sin(turn)
        bits = lax.shift_right_logical(gammas_ref[op], 2)
        for flag in range(2):
            at = OPS * 12 + op * 2 + flag
            on = lax.shift_right_logical(gammas_ref[op], flag) & 1
            table_ref[at : at + 1, :] = jnp.full((1, 128), on, jnp.int32).astype(F32)
        for group in range(6):
            spin = jnp.full((1, 128), group, jnp.int32) if group < 4 else 2 * (group - 4) + lax.shift_right_logical(lane, 6)
            common = spin & bits
            parity = (common ^ lax.shift_right_logical(common, 1)) & 1
            sign = (1 - 2 * parity).astype(F32)
            at = (op * 6 + group) * 2
            table_ref[at : at + 1, :] = cosine * sign
            table_ref[at + 1 : at + 2, :] = sine * sign


def block_of(mask):
    return lax.shift_right_logical(lax.axis_index("space") ^ mask, 1)


def sort_kernel(mask, basis_ref, after_ref, far_ref, near_ref, done_ref, reads_ref, in_sems, done_sem):
    step = 128
    chunks = 2 * WIDTH // step
    low = iota((step, 128), 1) < 64
    block = block_of(mask)
    core = lax.axis_index("space") & 1
    reads = []
    for chunk in range(chunks):
        rows = slice(chunk * step, (chunk + 1) * step)
        reads.append(pltpu.make_async_copy(basis_ref.at[block, rows, :], reads_ref.at[rows, :], in_sems.at[chunk]))
    for read in reads:
        read.start()
    for chunk, read in enumerate(reads):
        read.wait()
        if chunk == 0:
            done = pltpu.make_async_copy(reads_ref.at[:16, :128], done_ref, done_sem)
            done.start()
        rows = slice(chunk * step, (chunk + 1) * step)
        for out_ref, half in ((far_ref, 1 - core), (near_ref, core)):
            for group, (first, second) in enumerate(PAIRS):
                lanes = slice(group * 128, (group + 1) * 128)
                at = pl.multiple_of(half * 128, 128)
                a = reads_ref[rows, pl.ds(first * 256 + at, 128)]
                b = reads_ref[rows, pl.ds(second * 256 + at, 128)]
                out_ref[0, rows, lanes] = jnp.where(low, a, pltpu.roll(b, 64, 1))
                out_ref[1, rows, lanes] = jnp.where(low, pltpu.roll(a, 64, 1), b)
    done.wait()


def place(block, got_ref, placer_ref, coef_ref):
    for stop in range(STOPW):
        rows = got_ref[:, stop * 16 : (stop + 1) * 16, :].reshape(CAND, 2 * WIDTH)
        coef = jnp.dot(placer_ref[block, stop], rows, preferred_element_type=F32)
        re = coef[:, :WIDTH]
        im = coef[:, WIDTH:]
        top = slice(stop * MODES, (stop + 1) * MODES)
        bottom = slice(ROWS + stop * MODES, ROWS + (stop + 1) * MODES)
        coef_ref[top, :WIDTH] = re.astype(BF16)
        coef_ref[top, WIDTH:] = (-im).astype(BF16)
        coef_ref[bottom, :WIDTH] = im.astype(BF16)
        coef_ref[bottom, WIDTH:] = re.astype(BF16)


def entries(table_ref, coef_ref, slab, vec_ref, weight_ref):
    vec = jnp.dot(coef_ref[...], slab, preferred_element_type=F32).astype(BF16)
    vec_ref[:, :COLS] = vec[:ROWS]
    vec_ref[:, COLS:] = vec[ROWS:]
    own = []
    for part in range(2):
        lanes = [slice(part * COLS + group * 128, part * COLS + (group + 1) * 128) for group in range(6)]
        own.append([vec_ref[0:MODES, at].astype(F32) for at in lanes])
    rolled = [[pltpu.roll(own[part][4 + half], 64, 1) for half in range(2)] for part in range(2)]
    for op in range(OPS):
        at = OPS * 12 + op * 2
        swap = jnp.broadcast_to(table_ref[at : at + 1, :], (MODES, 128)) > 0.5
        cross = jnp.broadcast_to(table_ref[at + 1 : at + 2, :], (MODES, 128)) > 0.5
        spun = []
        for part in range(2):
            v = own[part]
            r = rolled[part]
            crossed = [jnp.where(cross, v[spin ^ 2], v[spin]) for spin in range(4)]
            whole = [jnp.where(cross, v[4 + (half ^ 1)], v[4 + half]) for half in range(2)]
            turned = [jnp.where(cross, r[half ^ 1], r[half]) for half in range(2)]
            spun.append(
                [jnp.where(swap, crossed[spin ^ 1], crossed[spin]) for spin in range(4)]
                + [jnp.where(swap, turned[half], whole[half]) for half in range(2)]
            )
        for group in range(6):
            re = spun[0][group]
            im = spun[1][group]
            at = (op * 6 + group) * 2
            cosine = table_ref[at : at + 1, :]
            sine = table_ref[at + 1 : at + 2, :]
            w_re = cosine * re - sine * im
            w_im = sine * re + cosine * im
            real = slice(op * MODES, (op + 1) * MODES)
            imag = slice(128 + op * MODES, 128 + (op + 1) * MODES)
            left = slice(group * 128, (group + 1) * 128)
            right = slice(COLS + group * 128, COLS + (group + 1) * 128)
            weight_ref[real, left] = w_re.astype(BF16)
            weight_ref[real, right] = w_im.astype(BF16)
            weight_ref[imag, left] = (-w_im).astype(BF16)
            weight_ref[imag, right] = w_re.astype(BF16)
    return lax.dot_general(vec_ref[...], weight_ref[...], (((1,), (1,)), ((), ())), preferred_element_type=F32)


def first_kernel(mask, table_ref, got_ref, placer_ref, slab_ref, out_ref, coef_ref, *work):
    place(block_of(mask), got_ref, placer_ref, coef_ref)
    for t in range(2):
        out_ref[t] = entries(table_ref, coef_ref, slab_ref[t], *work[2 * t : 2 * t + 2]).astype(BF16)


def second_kernel(table_ref, coef_ref, slab_ref, out_ref, *work):
    for t in range(2):
        out_ref[t] = entries(table_ref, coef_ref, slab_ref[t], *work[2 * t : 2 * t + 2])


def pair_kernel(own_ref, other_ref, out_a_ref, out_b_ref):
    for t, out_ref in enumerate((out_a_ref, out_b_ref)):
        out_ref[...] = (own_ref[t] + other_ref[t].astype(F32)).astype(BF16)


def last_kernel(table_ref, got_ref, placer_ref, far_ref, near_ref, before_ref, part_a_ref, part_b_ref, own_ref, coef_ref, *work):
    place(block_of(0), got_ref, placer_ref, coef_ref)
    for t, part_ref in enumerate((part_a_ref, part_b_ref)):
        part_ref[...] = entries(table_ref, coef_ref, far_ref[t], *work[2 * t : 2 * t + 2]).astype(BF16)
    for t in range(2):
        own_ref[t] = entries(table_ref, coef_ref, near_ref[t], *work[2 * t : 2 * t + 2])


def total_kernel(own_ref, near_a_ref, near_b_ref, far_a_ref, far_b_ref, out_ref, total_ref, sems):
    copies = []
    for t, (near_ref, far_ref) in enumerate(((near_a_ref, far_a_ref), (near_b_ref, far_b_ref))):
        total = own_ref[t] + near_ref[...].astype(F32) + far_ref[...].astype(F32)
        for op in range(OPS):
            for r in range(2):
                at = (r * OPS + op) * MODES
                total_ref[t, op, r] = total[:, at : at + MODES].reshape(STOPW, MODES, MODES)
            copy = pltpu.make_async_copy(total_ref.at[t, op], out_ref.at[t, op], sems.at[t, op])
            copy.start()
            copies.append(copy)
    for copy in copies:
        copy.wait()


VMEM = pl.BlockSpec(memory_space=pltpu.VMEM)
SMEM = pl.BlockSpec(memory_space=pltpu.SMEM)
HBM = pl.BlockSpec(memory_space=pltpu.HBM)
DMA = pltpu.SemaphoreType.DMA


def kernel_call(kernel, out_shape, in_specs, flops, moved, scratch=(), limit=8, out_specs=None):
    many = isinstance(out_shape, tuple)
    return pl.pallas_call(
        kernel,
        out_shape=out_shape,
        in_specs=in_specs,
        out_specs=out_specs or ((VMEM,) * len(out_shape) if many else VMEM),
        scratch_shapes=list(scratch),
        compiler_params=pltpu.CompilerParams(vmem_limit_bytes=limit * 1024 * 1024),
        cost_estimate=pl.CostEstimate(flops=flops, bytes_accessed=moved, transcendentals=0),
    )


def shape(dims, dtype=BF16):
    return jax.ShapeDtypeStruct(dims, dtype)


def per_device(coefs, counts, route, basis, momenta, gammas):
    packed = kernel_call(
        pack_kernel, shape((PLANES * 32, 2 * WIDTH)), [VMEM] * 3, 20_000_000, 400_000, limit=60
    )(route.reshape(32, 128), coefs.reshape(ITEMS, 2, WIDTH), counts.reshape(1, ITEMS))
    first = lax.all_to_all(
        packed.reshape(PLANES, 32, 2 * WIDTH), "mode", 0, 0, tiled=True, axis_index_groups=Z_GROUPS
    )
    by_reader = route.reshape(PLANES, SPOTS, ITEMS).transpose(2, 1, 0).reshape(ITEMS, 64)
    by_reader = jnp.repeat(by_reader, 2, axis=1)
    placer, table = kernel_call(
        tables_kernel,
        (shape((2, STOPW, MODES, CAND)), shape((OPS * 14, 128), F32)),
        [SMEM, SMEM, VMEM],
        2_000_000,
        200_000,
    )(momenta, gammas, by_reader)
    slab_shape = shape((2, 2 * WIDTH, COLS))
    token = shape((16, 128))

    def sort(mask, after, limit):
        return kernel_call(
            functools.partial(sort_kernel, mask),
            (slab_shape, slab_shape, token),
            [HBM, HBM],
            5_000_000,
            6_000_000,
            [pltpu.VMEM((2 * WIDTH, 4 * COLS), BF16), DMA((4,)), DMA],
            limit=limit,
            out_specs=(VMEM, VMEM, HBM),
        )(basis.reshape(2, 2 * WIDTH, 4 * COLS), after)

    slab_3, slab_2, done = sort(2, table, 52)
    onward = kernel_call(
        forward_kernel,
        shape((SPOTS, STOPW * 16, 2 * WIDTH)),
        [VMEM, HBM, VMEM],
        70_000_000,
        1_200_000,
        [pltpu.VMEM(((SPOTS + STOPW - 1) * 16, 2 * WIDTH), BF16), DMA((SPOTS,))],
        out_specs=HBM,
    )(first.reshape(PLANES * 32, 2 * WIDTH), done, table)
    got = lax.all_to_all(onward, "mode", 0, 0, tiled=True, axis_index_groups=P_GROUPS)
    slab_1, slab_0, _ = sort(0, onward, 59)
    got, slab_1, slab_0 = lax.optimization_barrier((got, slab_1, slab_0))
    part_shape = shape((ROWS, 256))
    pair_shape = shape((2, ROWS, 256))
    wide_shape = shape((2, ROWS, 256), F32)
    coef_shape = (2 * ROWS, 2 * WIDTH)
    work = [pltpu.VMEM((ROWS, 2 * COLS), BF16), pltpu.VMEM((256, 2 * COLS), BF16)] * 2

    def between(pair, part):
        return lax.ppermute(part, "space", [(i, i ^ pair) for i in range(4)])

    part_3, coef = kernel_call(
        functools.partial(first_kernel, 3),
        (pair_shape, shape(coef_shape)),
        [VMEM] * 4,
        1_200_000_000,
        3_000_000,
        work,
    )(table, got, placer, slab_3)
    part_2 = kernel_call(second_kernel, wide_shape, [VMEM] * 3, 1_100_000_000, 3_000_000, work)(table, coef, slab_2)
    chip_a, chip_b = kernel_call(pair_kernel, (part_shape, part_shape), [VMEM] * 2, 200_000, 900_000)(
        part_2, between(1, part_3)
    )
    far_a = between(2, chip_a)
    far_b = between(2, chip_b)
    part_a, part_b, own = kernel_call(
        last_kernel,
        (part_shape, part_shape, wide_shape),
        [VMEM] * 6,
        2_200_000_000,
        6_000_000,
        [pltpu.VMEM(coef_shape, BF16)] + work,
    )(table, got, placer, slab_1, slab_0, chip_b)
    part_a, part_b, far_a = lax.optimization_barrier((part_a, part_b, far_a))
    near_a = between(1, part_a)
    near_b = between(1, part_b)
    return kernel_call(
        total_kernel,
        shape((2, OPS, 2, STOPW, MODES, MODES), F32),
        [VMEM] * 5,
        1_000_000,
        3_000_000,
        [pltpu.VMEM((2, OPS, 2, STOPW, MODES, MODES), F32), DMA((2, OPS))],
        out_specs=HBM,
    )(own, near_a, near_b, far_a, far_b)


def solution(mesh):
    in_specs = (
        P("mode", "space", None, None),
        P("mode", "space"),
        P(),
        P("space", None, None, None),
        P(),
        P(),
    )
    out_specs = P("space", None, None, None, None, "mode")
    return jax.shard_map(
        per_device, mesh=mesh, in_specs=in_specs, out_specs=out_specs, check_vma=False
    )
```

```python
import functools
import math

import jax
import jax.numpy as jnp
from jax import lax
from jax.experimental import pallas as pl
from jax.experimental.pallas import tpu as pltpu
from jax.sharding import PartitionSpec as P

LAT = 64
STOPW = 7
PLANES = 8
SPOTS = 8
ITEMS = 64
WIDTH = 256
MODES = 32
ROWS = STOPW * MODES
COLS = 768
OPS = 4
CAND = 128
Z_GROUPS = [[z * SPOTS + p for z in range(PLANES)] for p in range(SPOTS)]
P_GROUPS = [[z * SPOTS + p for p in range(SPOTS)] for z in range(PLANES)]
PAIRS = [(0, 1), (3, 4), (6, 7), (9, 10), (2, 5), (8, 11)]
BF16 = jnp.bfloat16
F32 = jnp.float32


def iota(shape, axis):
    return lax.broadcasted_iota(jnp.int32, shape, axis)


def pack_kernel(route_ref, coefs_ref, counts_ref, out_ref):
    me = lax.axis_index("mode")
    row = route_ref[pl.ds(me // 2, 1), :]
    row = jnp.where(me % 2 == 1, pltpu.roll(row, 64, 1), row)[:, :ITEMS]
    owner = lax.shift_right_logical(row, 6)
    i = iota((ITEMS, ITEMS), 0)
    j = iota((ITEMS, ITEMS), 1)
    owners = jnp.broadcast_to(owner, (ITEMS, ITEMS)).astype(F32)
    column = jnp.sum(jnp.where(i == j, owners, 0.0), axis=1, keepdims=True)
    earlier = jnp.where((owners == column) & (i < j), 1.0, 0.0)
    rank = jnp.max(earlier, axis=0, keepdims=True).astype(jnp.int32)
    target = owner * 2 + rank
    q = iota((PLANES * 32, ITEMS), 0)
    plane = (lax.shift_right_logical(q, 5) - (lax.shift_right_logical(q, 4) & 1)) & 7
    want = plane * 16 + (q & 15)
    outgoing = jnp.where(want == target, 1.0, 0.0).astype(BF16)
    counts = jnp.broadcast_to(counts_ref[...], (ITEMS, ITEMS)).astype(F32)
    limit = jnp.sum(jnp.where(i == j, counts, 0.0), axis=1, keepdims=True).astype(jnp.int32)
    keep = iota((ITEMS, WIDTH), 1) < limit
    for part in range(2):
        block = jnp.where(keep, coefs_ref[:, part, :].astype(F32), 0.0).astype(BF16)
        packed = jnp.dot(outgoing, block, preferred_element_type=F32)
        out_ref[:, part * WIDTH : (part + 1) * WIDTH] = packed.astype(BF16)


def forward_kernel(got_ref, done_ref, out_ref, sorted_ref, sems):
    n = (SPOTS + STOPW - 1) * 16
    row = iota((n, PLANES * 32), 0)
    col = iota((n, PLANES * 32), 1)
    block = (SPOTS - 1 - lax.shift_right_logical(row, 4)) & 15
    source = (lax.shift_right_logical(row, 1) & 7) * 32 + block * 2 + (row & 1)
    order = jnp.where(col == source, 1.0, 0.0).astype(BF16)
    sorted_ref[...] = jnp.dot(order, got_ref[...], preferred_element_type=F32).astype(BF16)
    copies = []
    for spot in range(SPOTS):
        at = (SPOTS - 1 - spot) * 16
        copies.append(pltpu.make_async_copy(sorted_ref.at[at : at + STOPW * 16], out_ref.at[spot], sems.at[spot]))
    for copy in copies:
        copy.start()
    for copy in copies:
        copy.wait()


def tables_kernel(momenta_ref, gammas_ref, route_ref, after_ref, placer_ref, table_ref):
    me = lax.axis_index("mode")
    route = route_ref[...]
    owner = lax.shift_right_logical(route, 6)
    key = iota(route.shape, 0) * ITEMS + (route & (ITEMS - 1))
    keyf = key.astype(F32)
    second = (iota((1, CAND), 1) & 1) == 1
    mode = iota((MODES, CAND), 0)
    for stop in range(STOPW):
        hit = owner == ((me - stop) & 63)
        low = jnp.min(jnp.where(hit, keyf, 8192.0), axis=0, keepdims=True)
        high = jnp.max(jnp.where(hit, keyf, -1.0), axis=0, keepdims=True)
        valid = jnp.where(second, high - low, 8000.0 - low) > 0.0
        item = jnp.where(second, high, low).astype(jnp.int32) & (ITEMS - 1)
        item = jnp.where(valid, item, -1)
        for block in range(2):
            placer_ref[block, stop] = jnp.where(mode * 2 + block == item, 1.0, 0.0).astype(BF16)
    place = lax.axis_index("space")
    lane = iota((1, 128), 1)
    site = place * 64 + (lane & 63)
    xs = site & 3
    ys = lax.shift_right_logical(site, 2) & 3
    zs = lax.shift_right_logical(site, 4)
    for op in range(OPS):
        inner = momenta_ref[op, 0] * xs + momenta_ref[op, 1] * ys + momenta_ref[op, 2] * zs
        turn = inner.astype(F32) * (2.0 * math.pi / LAT)
        cosine = jnp.cos(turn)
        sine = jnp.sin(turn)
        bits = lax.shift_right_logical(gammas_ref[op], 2)
        for flag in range(2):
            at = OPS * 12 + op * 2 + flag
            on = lax.shift_right_logical(gammas_ref[op], flag) & 1
            table_ref[at : at + 1, :] = jnp.full((1, 128), on, jnp.int32).astype(F32)
        for group in range(6):
            spin = jnp.full((1, 128), group, jnp.int32) if group < 4 else 2 * (group - 4) + lax.shift_right_logical(lane, 6)
            common = spin & bits
            parity = (common ^ lax.shift_right_logical(common, 1)) & 1
            sign = (1 - 2 * parity).astype(F32)
            at = (op * 6 + group) * 2
            table_ref[at : at + 1, :] = cosine * sign
            table_ref[at + 1 : at + 2, :] = sine * sign


def block_of(mask):
    return lax.shift_right_logical(lax.axis_index("space") ^ mask, 1)


def sort_kernel(mask, basis_ref, *rest):
    far_ref, near_ref, done_ref, reads_ref, in_sems, done_sem = rest[-6:]
    step = 128
    chunks = 2 * WIDTH // step
    low = iota((step, 128), 1) < 64
    block = block_of(mask)
    core = lax.axis_index("space") & 1
    reads = []
    for chunk in range(chunks):
        rows = slice(chunk * step, (chunk + 1) * step)
        reads.append(pltpu.make_async_copy(basis_ref.at[block, rows, :], reads_ref.at[rows, :], in_sems.at[chunk]))
    for read in reads:
        read.start()
    for chunk, read in enumerate(reads):
        read.wait()
        if chunk == 0:
            done = pltpu.make_async_copy(reads_ref.at[:16, :128], done_ref, done_sem)
            done.start()
        rows = slice(chunk * step, (chunk + 1) * step)
        for out_ref, half in ((far_ref, 1 - core), (near_ref, core)):
            for group, (first, second) in enumerate(PAIRS):
                lanes = slice(group * 128, (group + 1) * 128)
                at = pl.multiple_of(half * 128, 128)
                a = reads_ref[rows, pl.ds(first * 256 + at, 128)]
                b = reads_ref[rows, pl.ds(second * 256 + at, 128)]
                out_ref[0, rows, lanes] = jnp.where(low, a, pltpu.roll(b, 64, 1))
                out_ref[1, rows, lanes] = jnp.where(low, pltpu.roll(a, 64, 1), b)
    done.wait()


def place(block, got_ref, placer_ref, coef_ref):
    for stop in range(STOPW):
        rows = got_ref[:, stop * 16 : (stop + 1) * 16, :].reshape(CAND, 2 * WIDTH)
        coef = jnp.dot(placer_ref[block, stop], rows, preferred_element_type=F32)
        re = coef[:, :WIDTH]
        im = coef[:, WIDTH:]
        top = slice(stop * MODES, (stop + 1) * MODES)
        bottom = slice(ROWS + stop * MODES, ROWS + (stop + 1) * MODES)
        coef_ref[top, :WIDTH] = re.astype(BF16)
        coef_ref[top, WIDTH:] = (-im).astype(BF16)
        coef_ref[bottom, :WIDTH] = im.astype(BF16)
        coef_ref[bottom, WIDTH:] = re.astype(BF16)


def expand(coef_ref, slab, vec_ref, chunk):
    lanes = slice(chunk * 256, (chunk + 1) * 256)
    vec = jnp.dot(coef_ref[...], slab[:, lanes], preferred_element_type=F32).astype(BF16)
    vec_ref[:, lanes] = vec[:ROWS]
    vec_ref[:, COLS + chunk * 256 : COLS + (chunk + 1) * 256] = vec[ROWS:]


def weigh(op, table_ref, vec_ref, weight_ref):
    at = OPS * 12 + op * 2
    swap = jnp.broadcast_to(table_ref[at : at + 1, :], (MODES, 128)) > 0.5
    cross = jnp.broadcast_to(table_ref[at + 1 : at + 2, :], (MODES, 128)) > 0.5
    spun = []
    for part in range(2):
        lanes = [slice(part * COLS + group * 128, part * COLS + (group + 1) * 128) for group in range(6)]
        v = [vec_ref[0:MODES, at].astype(F32) for at in lanes]
        r = [pltpu.roll(v[4 + half], 64, 1) for half in range(2)]
        crossed = [jnp.where(cross, v[spin ^ 2], v[spin]) for spin in range(4)]
        whole = [jnp.where(cross, v[4 + (half ^ 1)], v[4 + half]) for half in range(2)]
        turned = [jnp.where(cross, r[half ^ 1], r[half]) for half in range(2)]
        spun.append(
            [jnp.where(swap, crossed[spin ^ 1], crossed[spin]) for spin in range(4)]
            + [jnp.where(swap, turned[half], whole[half]) for half in range(2)]
        )
    for group in range(6):
        re = spun[0][group]
        im = spun[1][group]
        at = (op * 6 + group) * 2
        cosine = table_ref[at : at + 1, :]
        sine = table_ref[at + 1 : at + 2, :]
        w_re = cosine * re - sine * im
        w_im = sine * re + cosine * im
        real = slice(op * MODES, (op + 1) * MODES)
        imag = slice(128 + op * MODES, 128 + (op + 1) * MODES)
        left = slice(group * 128, (group + 1) * 128)
        right = slice(COLS + group * 128, COLS + (group + 1) * 128)
        weight_ref[real, left] = w_re.astype(BF16)
        weight_ref[real, right] = w_im.astype(BF16)
        weight_ref[imag, left] = (-w_im).astype(BF16)
        weight_ref[imag, right] = w_re.astype(BF16)


def contract(vec_ref, weight_ref, third):
    lanes = slice(third * 512, (third + 1) * 512)
    return lax.dot_general(
        vec_ref[:, lanes], weight_ref[:, lanes], (((1,), (1,)), ((), ())), preferred_element_type=F32
    )


def entries(table_ref, coef_ref, slab_ref, store, vec_0, weight_0, vec_1, weight_1):
    for chunk in range(3):
        expand(coef_ref, slab_ref[0], vec_0, chunk)
    for op in range(OPS):
        weigh(op, table_ref, vec_0, weight_0)
        if op < 3:
            expand(coef_ref, slab_ref[1], vec_1, op)
    total = None
    for op in range(OPS):
        if op < 3:
            part = contract(vec_0, weight_0, op)
            total = part if total is None else total + part
        weigh(op, table_ref, vec_1, weight_1)
    store(0, total)
    store(1, sum(contract(vec_1, weight_1, third) for third in range(3)))


def put(*refs):
    def store(t, total):
        refs[t][...] = total.astype(refs[t].dtype)

    return store


def first_kernel(mask, table_ref, got_ref, placer_ref, slab_ref, out_ref, coef_ref, *work):
    place(block_of(mask), got_ref, placer_ref, coef_ref)
    entries(table_ref, coef_ref, slab_ref, put(out_ref.at[0], out_ref.at[1]), *work)


def second_kernel(table_ref, coef_ref, slab_ref, out_ref, *work):
    entries(table_ref, coef_ref, slab_ref, put(out_ref.at[0], out_ref.at[1]), *work)


def pair_kernel(own_ref, other_ref, out_a_ref, out_b_ref):
    for t, out_ref in enumerate((out_a_ref, out_b_ref)):
        out_ref[...] = (own_ref[t] + other_ref[t].astype(F32)).astype(BF16)


def last_kernel(table_ref, got_ref, placer_ref, far_ref, near_ref, before_ref, part_a_ref, part_b_ref, own_ref, coef_ref, *work):
    place(block_of(0), got_ref, placer_ref, coef_ref)
    entries(table_ref, coef_ref, far_ref, put(part_a_ref, part_b_ref), *work)
    entries(table_ref, coef_ref, near_ref, put(own_ref.at[0], own_ref.at[1]), *work)


def total_kernel(own_ref, near_a_ref, near_b_ref, far_a_ref, far_b_ref, out_ref, total_ref, sems):
    copies = []
    for t, (near_ref, far_ref) in enumerate(((near_a_ref, far_a_ref), (near_b_ref, far_b_ref))):
        total = own_ref[t] + near_ref[...].astype(F32) + far_ref[...].astype(F32)
        for op in range(OPS):
            for r in range(2):
                at = (r * OPS + op) * MODES
                total_ref[t, op, r] = total[:, at : at + MODES].reshape(STOPW, MODES, MODES)
            copy = pltpu.make_async_copy(total_ref.at[t, op], out_ref.at[t, op], sems.at[t, op])
            copy.start()
            copies.append(copy)
    for copy in copies:
        copy.wait()


VMEM = pl.BlockSpec(memory_space=pltpu.VMEM)
SMEM = pl.BlockSpec(memory_space=pltpu.SMEM)
HBM = pl.BlockSpec(memory_space=pltpu.HBM)
DMA = pltpu.SemaphoreType.DMA


def kernel_call(kernel, out_shape, in_specs, flops, moved, scratch=(), limit=8, out_specs=None):
    many = isinstance(out_shape, tuple)
    return pl.pallas_call(
        kernel,
        out_shape=out_shape,
        in_specs=in_specs,
        out_specs=out_specs or ((VMEM,) * len(out_shape) if many else VMEM),
        scratch_shapes=list(scratch),
        compiler_params=pltpu.CompilerParams(vmem_limit_bytes=limit * 1024 * 1024),
        cost_estimate=pl.CostEstimate(flops=flops, bytes_accessed=moved, transcendentals=0),
    )


def shape(dims, dtype=BF16):
    return jax.ShapeDtypeStruct(dims, dtype)


def per_device(coefs, counts, route, basis, momenta, gammas):
    packed = kernel_call(
        pack_kernel, shape((PLANES * 32, 2 * WIDTH)), [VMEM] * 3, 20_000_000, 400_000, limit=60
    )(route.reshape(32, 128), coefs.reshape(ITEMS, 2, WIDTH), counts.reshape(1, ITEMS))
    first = lax.all_to_all(
        packed.reshape(PLANES, 32, 2 * WIDTH), "mode", 0, 0, tiled=True, axis_index_groups=Z_GROUPS
    )
    slab_shape = shape((2, 2 * WIDTH, COLS))
    token = shape((16, 128))

    def sort(mask, limit, *after):
        return kernel_call(
            functools.partial(sort_kernel, mask),
            (slab_shape, slab_shape, token),
            [HBM] * (1 + len(after)),
            5_000_000,
            6_000_000,
            [pltpu.VMEM((2 * WIDTH, 4 * COLS), BF16), DMA((4,)), DMA],
            limit=limit,
            out_specs=(VMEM, VMEM, HBM),
        )(basis.reshape(2, 2 * WIDTH, 4 * COLS), *after)

    slab_3, slab_2, done = sort(2, 52)
    onward = kernel_call(
        forward_kernel,
        shape((SPOTS, STOPW * 16, 2 * WIDTH)),
        [VMEM, HBM],
        70_000_000,
        1_200_000,
        [pltpu.VMEM(((SPOTS + STOPW - 1) * 16, 2 * WIDTH), BF16), DMA((SPOTS,))],
        out_specs=HBM,
    )(first.reshape(PLANES * 32, 2 * WIDTH), done)
    by_reader = route.reshape(PLANES, SPOTS, ITEMS).transpose(2, 1, 0).reshape(ITEMS, 64)
    by_reader = jnp.repeat(by_reader, 2, axis=1)
    placer, table = kernel_call(
        tables_kernel,
        (shape((2, STOPW, MODES, CAND)), shape((OPS * 14, 128), F32)),
        [SMEM, SMEM, VMEM, HBM],
        2_000_000,
        200_000,
    )(momenta, gammas, by_reader, onward)
    got = lax.all_to_all(onward, "mode", 0, 0, tiled=True, axis_index_groups=P_GROUPS)
    slab_1, slab_0, _ = sort(0, 59, onward)
    got, slab_1, slab_0 = lax.optimization_barrier((got, slab_1, slab_0))
    part_shape = shape((ROWS, 256))
    pair_shape = shape((2, ROWS, 256))
    wide_shape = shape((2, ROWS, 256), F32)
    coef_shape = (2 * ROWS, 2 * WIDTH)
    work = [pltpu.VMEM((ROWS, 2 * COLS), BF16), pltpu.VMEM((256, 2 * COLS), BF16)] * 2

    def between(pair, part):
        return lax.ppermute(part, "space", [(i, i ^ pair) for i in range(4)])

    part_3, coef = kernel_call(
        functools.partial(first_kernel, 3),
        (pair_shape, shape(coef_shape)),
        [VMEM] * 4,
        1_200_000_000,
        3_000_000,
        work,
    )(table, got, placer, slab_3)
    part_2 = kernel_call(second_kernel, wide_shape, [VMEM] * 3, 1_100_000_000, 3_000_000, work)(table, coef, slab_2)
    chip_a, chip_b = kernel_call(pair_kernel, (part_shape, part_shape), [VMEM] * 2, 200_000, 900_000)(
        part_2, between(1, part_3)
    )
    far_a = between(2, chip_a)
    far_b = between(2, chip_b)
    part_a, part_b, own = kernel_call(
        last_kernel,
        (part_shape, part_shape, wide_shape),
        [VMEM] * 6,
        2_200_000_000,
        6_000_000,
        [pltpu.VMEM(coef_shape, BF16)] + work,
    )(table, got, placer, slab_1, slab_0, chip_b)
    part_a, part_b, far_a = lax.optimization_barrier((part_a, part_b, far_a))
    near_a = between(1, part_a)
    near_b = between(1, part_b)
    return kernel_call(
        total_kernel,
        shape((2, OPS, 2, STOPW, MODES, MODES), F32),
        [VMEM] * 5,
        1_000_000,
        3_000_000,
        [pltpu.VMEM((2, OPS, 2, STOPW, MODES, MODES), F32), DMA((2, OPS))],
        out_specs=HBM,
    )(own, near_a, near_b, far_a, far_b)


def solution(mesh):
    in_specs = (
        P("mode", "space", None, None),
        P("mode", "space"),
        P(),
        P("space", None, None, None),
        P(),
        P(),
    )
    out_specs = P("space", None, None, None, None, "mode")
    return jax.shard_map(
        per_device, mesh=mesh, in_specs=in_specs, out_specs=out_specs, check_vma=False
    )
```

```python
import functools
import math

import jax
import jax.numpy as jnp
from jax import lax
from jax.experimental import pallas as pl
from jax.experimental.pallas import tpu as pltpu
from jax.sharding import PartitionSpec as P

LAT = 64
STOPW = 7
PLANES = 8
SPOTS = 8
ITEMS = 64
WIDTH = 256
MODES = 32
ROWS = STOPW * MODES
COLS = 768
OPS = 4
CAND = 128
Z_GROUPS = [[z * SPOTS + p for z in range(PLANES)] for p in range(SPOTS)]
P_GROUPS = [[z * SPOTS + p for p in range(SPOTS)] for z in range(PLANES)]
PAIRS = [(0, 1), (3, 4), (6, 7), (9, 10), (2, 5), (8, 11)]
BF16 = jnp.bfloat16
F32 = jnp.float32


def iota(shape, axis):
    return lax.broadcasted_iota(jnp.int32, shape, axis)


def pack_kernel(route_in, coefs_in, counts_in, out_hbm, route_ref, coefs_ref, counts_ref, out_ref, sems, out_sems):
    reads = [
        pltpu.make_async_copy(source, target, sems.at[n])
        for n, (source, target) in enumerate(
            ((route_in, route_ref), (counts_in, counts_ref), (coefs_in, coefs_ref))
        )
    ]
    for read in reads:
        read.start()
    reads[0].wait()
    me = lax.axis_index("mode")
    row = route_ref[pl.ds(me // 2, 1), :]
    row = jnp.where(me % 2 == 1, pltpu.roll(row, 64, 1), row)[:, :ITEMS]
    owner = lax.shift_right_logical(row, 6)
    i = iota((ITEMS, ITEMS), 0)
    j = iota((ITEMS, ITEMS), 1)
    owners = jnp.broadcast_to(owner, (ITEMS, ITEMS)).astype(F32)
    column = jnp.sum(jnp.where(i == j, owners, 0.0), axis=1, keepdims=True)
    earlier = jnp.where((owners == column) & (i < j), 1.0, 0.0)
    rank = jnp.max(earlier, axis=0, keepdims=True).astype(jnp.int32)
    target = owner * 2 + rank
    q = iota((PLANES * 32, ITEMS), 0)
    plane = (lax.shift_right_logical(q, 5) - (lax.shift_right_logical(q, 4) & 1)) & 7
    want = plane * 16 + (q & 15)
    outgoing = jnp.where(want == target, 1.0, 0.0).astype(BF16)
    reads[1].wait()
    counts = jnp.broadcast_to(counts_ref[...], (ITEMS, ITEMS)).astype(F32)
    limit = jnp.sum(jnp.where(i == j, counts, 0.0), axis=1, keepdims=True).astype(jnp.int32)
    keep = iota((ITEMS, WIDTH), 1) < limit
    reads[2].wait()
    blocks = [jnp.where(keep, coefs_ref[:, part, :].astype(F32), 0.0).astype(BF16) for part in range(2)]
    writes = []
    for half in range(2):
        rows = slice(half * 128, (half + 1) * 128)
        for part in range(2):
            packed = jnp.dot(outgoing[rows], blocks[part], preferred_element_type=F32)
            out_ref[rows, part * WIDTH : (part + 1) * WIDTH] = packed.astype(BF16)
        write = pltpu.make_async_copy(out_ref.at[rows], out_hbm.at[rows], out_sems.at[half])
        write.start()
        writes.append(write)
    for write in writes:
        write.wait()


def forward_kernel(got_ref, done_ref, out_ref, sorted_ref, sems):
    n = (SPOTS + STOPW - 1) * 16
    row = iota((n, PLANES * 32), 0)
    col = iota((n, PLANES * 32), 1)
    block = (SPOTS - 1 - lax.shift_right_logical(row, 4)) & 15
    source = (lax.shift_right_logical(row, 1) & 7) * 32 + block * 2 + (row & 1)
    order = jnp.where(col == source, 1.0, 0.0).astype(BF16)
    sorted_ref[...] = jnp.dot(order, got_ref[...], preferred_element_type=F32).astype(BF16)
    copies = []
    for spot in range(SPOTS):
        at = (SPOTS - 1 - spot) * 16
        copies.append(pltpu.make_async_copy(sorted_ref.at[at : at + STOPW * 16], out_ref.at[spot], sems.at[spot]))
    for copy in copies:
        copy.start()
    for copy in copies:
        copy.wait()


def tables_kernel(momenta_ref, gammas_ref, route_ref, after_ref, placer_ref, table_ref):
    me = lax.axis_index("mode")
    route = route_ref[...]
    owner = lax.shift_right_logical(route, 6)
    key = iota(route.shape, 0) * ITEMS + (route & (ITEMS - 1))
    keyf = key.astype(F32)
    second = (iota((1, CAND), 1) & 1) == 1
    mode = iota((MODES, CAND), 0)
    for stop in range(STOPW):
        hit = owner == ((me - stop) & 63)
        low = jnp.min(jnp.where(hit, keyf, 8192.0), axis=0, keepdims=True)
        high = jnp.max(jnp.where(hit, keyf, -1.0), axis=0, keepdims=True)
        valid = jnp.where(second, high - low, 8000.0 - low) > 0.0
        item = jnp.where(second, high, low).astype(jnp.int32) & (ITEMS - 1)
        item = jnp.where(valid, item, -1)
        for block in range(2):
            placer_ref[block, stop] = jnp.where(mode * 2 + block == item, 1.0, 0.0).astype(BF16)
    place = lax.axis_index("space")
    lane = iota((1, 128), 1)
    site = place * 64 + (lane & 63)
    xs = site & 3
    ys = lax.shift_right_logical(site, 2) & 3
    zs = lax.shift_right_logical(site, 4)
    for op in range(OPS):
        inner = momenta_ref[op, 0] * xs + momenta_ref[op, 1] * ys + momenta_ref[op, 2] * zs
        turn = inner.astype(F32) * (2.0 * math.pi / LAT)
        cosine = jnp.cos(turn)
        sine = jnp.sin(turn)
        bits = lax.shift_right_logical(gammas_ref[op], 2)
        for flag in range(2):
            at = OPS * 12 + op * 2 + flag
            on = lax.shift_right_logical(gammas_ref[op], flag) & 1
            table_ref[at : at + 1, :] = jnp.full((1, 128), on, jnp.int32).astype(F32)
        for group in range(6):
            spin = jnp.full((1, 128), group, jnp.int32) if group < 4 else 2 * (group - 4) + lax.shift_right_logical(lane, 6)
            common = spin & bits
            parity = (common ^ lax.shift_right_logical(common, 1)) & 1
            sign = (1 - 2 * parity).astype(F32)
            at = (op * 6 + group) * 2
            table_ref[at : at + 1, :] = cosine * sign
            table_ref[at + 1 : at + 2, :] = sine * sign


def block_of(mask):
    return lax.shift_right_logical(lax.axis_index("space") ^ mask, 1)


def sort_kernel(mask, basis_ref, *rest):
    far_ref, near_ref, done_ref, reads_ref, in_sems, done_sem = rest[-6:]
    odd_far_ref, odd_near_ref = (near_ref, far_ref) if mask == 2 else (far_ref, near_ref)
    step = 128
    chunks = 2 * WIDTH // step
    low = iota((step, 128), 1) < 64
    block = block_of(mask)
    core = lax.axis_index("space") & 1
    reads = []
    for chunk in range(chunks):
        rows = slice(chunk * step, (chunk + 1) * step)
        reads.append(pltpu.make_async_copy(basis_ref.at[block, rows, :], reads_ref.at[rows, :], in_sems.at[chunk]))
    for read in reads:
        read.start()
    for chunk, read in enumerate(reads):
        read.wait()
        if chunk == 0:
            done = pltpu.make_async_copy(reads_ref.at[:16, :128], done_ref, done_sem)
            done.start()
        rows = slice(chunk * step, (chunk + 1) * step)
        for even_ref, odd_ref, half in ((far_ref, odd_far_ref, 1 - core), (near_ref, odd_near_ref, core)):
            for group, (first, second) in enumerate(PAIRS):
                lanes = slice(group * 128, (group + 1) * 128)
                at = pl.multiple_of(half * 128, 128)
                a = reads_ref[rows, pl.ds(first * 256 + at, 128)]
                b = reads_ref[rows, pl.ds(second * 256 + at, 128)]
                even_ref[0, rows, lanes] = jnp.where(low, a, pltpu.roll(b, 64, 1))
                odd_ref[1, rows, lanes] = jnp.where(low, pltpu.roll(a, 64, 1), b)
    done.wait()


def place(block, got_ref, placer_ref, coef_ref):
    for stop in range(STOPW):
        rows = got_ref[:, stop * 16 : (stop + 1) * 16, :].reshape(CAND, 2 * WIDTH)
        coef = jnp.dot(placer_ref[block, stop], rows, preferred_element_type=F32)
        re = coef[:, :WIDTH]
        im = coef[:, WIDTH:]
        top = slice(stop * MODES, (stop + 1) * MODES)
        bottom = slice(ROWS + stop * MODES, ROWS + (stop + 1) * MODES)
        coef_ref[top, :WIDTH] = re.astype(BF16)
        coef_ref[top, WIDTH:] = (-im).astype(BF16)
        coef_ref[bottom, :WIDTH] = im.astype(BF16)
        coef_ref[bottom, WIDTH:] = re.astype(BF16)


def expand(coef_ref, slab, vec_ref, chunk):
    lanes = slice(chunk * 256, (chunk + 1) * 256)
    vec = jnp.dot(coef_ref[...], slab[:, lanes], preferred_element_type=F32).astype(BF16)
    vec_ref[:, lanes] = vec[:ROWS]
    vec_ref[:, COLS + chunk * 256 : COLS + (chunk + 1) * 256] = vec[ROWS:]


def weigh(op, table_ref, vec_ref, weight_ref):
    at = OPS * 12 + op * 2
    swap = jnp.broadcast_to(table_ref[at : at + 1, :], (MODES, 128)) > 0.5
    cross = jnp.broadcast_to(table_ref[at + 1 : at + 2, :], (MODES, 128)) > 0.5
    spun = []
    for part in range(2):
        lanes = [slice(part * COLS + group * 128, part * COLS + (group + 1) * 128) for group in range(6)]
        v = [vec_ref[0:MODES, at].astype(F32) for at in lanes]
        r = [pltpu.roll(v[4 + half], 64, 1) for half in range(2)]
        crossed = [jnp.where(cross, v[spin ^ 2], v[spin]) for spin in range(4)]
        whole = [jnp.where(cross, v[4 + (half ^ 1)], v[4 + half]) for half in range(2)]
        turned = [jnp.where(cross, r[half ^ 1], r[half]) for half in range(2)]
        spun.append(
            [jnp.where(swap, crossed[spin ^ 1], crossed[spin]) for spin in range(4)]
            + [jnp.where(swap, turned[half], whole[half]) for half in range(2)]
        )
    for group in range(6):
        re = spun[0][group]
        im = spun[1][group]
        at = (op * 6 + group) * 2
        cosine = table_ref[at : at + 1, :]
        sine = table_ref[at + 1 : at + 2, :]
        w_re = cosine * re - sine * im
        w_im = sine * re + cosine * im
        real = slice(op * MODES, (op + 1) * MODES)
        imag = slice(128 + op * MODES, 128 + (op + 1) * MODES)
        left = slice(group * 128, (group + 1) * 128)
        right = slice(COLS + group * 128, COLS + (group + 1) * 128)
        weight_ref[real, left] = w_re.astype(BF16)
        weight_ref[real, right] = w_im.astype(BF16)
        weight_ref[imag, left] = (-w_im).astype(BF16)
        weight_ref[imag, right] = w_re.astype(BF16)


def contract(vec_ref, weight_ref, third):
    lanes = slice(third * 512, (third + 1) * 512)
    return lax.dot_general(
        vec_ref[:, lanes], weight_ref[:, lanes], (((1,), (1,)), ((), ())), preferred_element_type=F32
    )


def entries(table_ref, coef_ref, slab_ref, store, vec_0, weight_0, vec_1, weight_1):
    for chunk in range(3):
        expand(coef_ref, slab_ref[0], vec_0, chunk)
    for op in range(OPS):
        weigh(op, table_ref, vec_0, weight_0)
        if op < 3:
            expand(coef_ref, slab_ref[1], vec_1, op)
    total = None
    for op in range(OPS):
        if op < 3:
            part = contract(vec_0, weight_0, op)
            total = part if total is None else total + part
        weigh(op, table_ref, vec_1, weight_1)
    store(0, total)
    store(1, sum(contract(vec_1, weight_1, third) for third in range(3)))


def put(*refs):
    def store(t, total):
        refs[t][...] = total.astype(refs[t].dtype)

    return store


def first_kernel(mask, table_ref, got_ref, placer_ref, slab_ref, out_ref, coef_ref, *work):
    place(block_of(mask), got_ref, placer_ref, coef_ref)
    entries(table_ref, coef_ref, slab_ref, put(out_ref.at[0], out_ref.at[1]), *work)


def second_kernel(table_ref, coef_ref, slab_ref, out_ref, *work):
    entries(table_ref, coef_ref, slab_ref, put(out_ref.at[0], out_ref.at[1]), *work)


def pair_kernel(own_ref, other_ref, out_a_ref, out_b_ref):
    for t, out_ref in enumerate((out_a_ref, out_b_ref)):
        out_ref[...] = (own_ref[t] + other_ref[t].astype(F32)).astype(BF16)


def last_kernel(table_ref, got_ref, placer_ref, far_ref, near_ref, before_ref, part_a_ref, part_b_ref, own_ref, coef_ref, *work):
    place(block_of(0), got_ref, placer_ref, coef_ref)
    entries(table_ref, coef_ref, far_ref, put(part_a_ref, part_b_ref), *work)
    entries(table_ref, coef_ref, near_ref, put(own_ref.at[0], own_ref.at[1]), *work)


def total_kernel(own_ref, near_a_ref, near_b_ref, far_a_ref, far_b_ref, out_ref, total_ref, sems):
    copies = []
    for t, (near_ref, far_ref) in enumerate(((near_a_ref, far_a_ref), (near_b_ref, far_b_ref))):
        total = own_ref[t] + near_ref[...].astype(F32) + far_ref[...].astype(F32)
        for op in range(OPS):
            for r in range(2):
                at = (r * OPS + op) * MODES
                total_ref[t, op, r] = total[:, at : at + MODES].reshape(STOPW, MODES, MODES)
            copy = pltpu.make_async_copy(total_ref.at[t, op], out_ref.at[t, op], sems.at[t, op])
            copy.start()
            copies.append(copy)
    for copy in copies:
        copy.wait()


VMEM = pl.BlockSpec(memory_space=pltpu.VMEM)
SMEM = pl.BlockSpec(memory_space=pltpu.SMEM)
HBM = pl.BlockSpec(memory_space=pltpu.HBM)
DMA = pltpu.SemaphoreType.DMA


def kernel_call(kernel, out_shape, in_specs, flops, moved, scratch=(), limit=8, out_specs=None):
    many = isinstance(out_shape, tuple)
    return pl.pallas_call(
        kernel,
        out_shape=out_shape,
        in_specs=in_specs,
        out_specs=out_specs or ((VMEM,) * len(out_shape) if many else VMEM),
        scratch_shapes=list(scratch),
        compiler_params=pltpu.CompilerParams(vmem_limit_bytes=limit * 1024 * 1024),
        cost_estimate=pl.CostEstimate(flops=flops, bytes_accessed=moved, transcendentals=0),
    )


def shape(dims, dtype=BF16):
    return jax.ShapeDtypeStruct(dims, dtype)


def per_device(coefs, counts, route, basis, momenta, gammas):
    packed = kernel_call(
        pack_kernel,
        shape((PLANES * 32, 2 * WIDTH)),
        [HBM] * 3,
        20_000_000,
        400_000,
        [
            pltpu.VMEM((32, 128), jnp.int32),
            pltpu.VMEM((ITEMS, 2, WIDTH), BF16),
            pltpu.VMEM((1, ITEMS), jnp.int32),
            pltpu.VMEM((PLANES * 32, 2 * WIDTH), BF16),
            DMA((3,)),
            DMA((2,)),
        ],
        limit=60,
        out_specs=HBM,
    )(route.reshape(32, 128), coefs.reshape(ITEMS, 2, WIDTH), counts.reshape(1, ITEMS))
    first = lax.all_to_all(
        packed.reshape(PLANES, 32, 2 * WIDTH), "mode", 0, 0, tiled=True, axis_index_groups=Z_GROUPS
    )
    slab_shape = shape((2, 2 * WIDTH, COLS))
    token = shape((16, 128))

    def sort(mask, limit, *after):
        return kernel_call(
            functools.partial(sort_kernel, mask),
            (slab_shape, slab_shape, token),
            [HBM] * (1 + len(after)),
            5_000_000,
            6_000_000,
            [pltpu.VMEM((2 * WIDTH, 4 * COLS), BF16), DMA((4,)), DMA],
            limit=limit,
            out_specs=(VMEM, VMEM, HBM),
        )(basis.reshape(2, 2 * WIDTH, 4 * COLS), *after)

    slab_3, slab_2, done = sort(2, 52)
    onward = kernel_call(
        forward_kernel,
        shape((SPOTS, STOPW * 16, 2 * WIDTH)),
        [VMEM, HBM],
        70_000_000,
        1_200_000,
        [pltpu.VMEM(((SPOTS + STOPW - 1) * 16, 2 * WIDTH), BF16), DMA((SPOTS,))],
        out_specs=HBM,
    )(first.reshape(PLANES * 32, 2 * WIDTH), done)
    by_reader = route.reshape(PLANES, SPOTS, ITEMS).transpose(2, 1, 0).reshape(ITEMS, 64)
    by_reader = jnp.repeat(by_reader, 2, axis=1)
    placer, table = kernel_call(
        tables_kernel,
        (shape((2, STOPW, MODES, CAND)), shape((OPS * 14, 128), F32)),
        [SMEM, SMEM, VMEM, HBM],
        2_000_000,
        200_000,
    )(momenta, gammas, by_reader, onward)
    got = lax.all_to_all(onward, "mode", 0, 0, tiled=True, axis_index_groups=P_GROUPS)
    slab_1, slab_0, _ = sort(0, 59, onward)
    got, slab_1, slab_0 = lax.optimization_barrier((got, slab_1, slab_0))
    part_shape = shape((ROWS, 256))
    pair_shape = shape((2, ROWS, 256))
    wide_shape = shape((2, ROWS, 256), F32)
    coef_shape = (2 * ROWS, 2 * WIDTH)
    work = [pltpu.VMEM((ROWS, 2 * COLS), BF16), pltpu.VMEM((256, 2 * COLS), BF16)] * 2

    def between(pair, part):
        return lax.ppermute(part, "space", [(i, i ^ pair) for i in range(4)])

    part_3, coef = kernel_call(
        functools.partial(first_kernel, 3),
        (pair_shape, shape(coef_shape)),
        [VMEM] * 4,
        1_200_000_000,
        3_000_000,
        work,
    )(table, got, placer, slab_3)
    part_2 = kernel_call(second_kernel, wide_shape, [VMEM] * 3, 1_100_000_000, 3_000_000, work)(table, coef, slab_2)
    chip_a, chip_b = kernel_call(pair_kernel, (part_shape, part_shape), [VMEM] * 2, 200_000, 900_000)(
        part_2, between(1, part_3)
    )
    far_a = between(2, chip_a)
    far_b = between(3, chip_b)
    part_a, part_b, own = kernel_call(
        last_kernel,
        (part_shape, part_shape, wide_shape),
        [VMEM] * 6,
        2_200_000_000,
        6_000_000,
        [pltpu.VMEM(coef_shape, BF16)] + work,
    )(table, got, placer, slab_1, slab_0, chip_b)
    part_a, part_b, far_a = lax.optimization_barrier((part_a, part_b, far_a))
    near_a = between(1, part_a)
    near_b = between(1, part_b)
    return kernel_call(
        total_kernel,
        shape((2, OPS, 2, STOPW, MODES, MODES), F32),
        [VMEM] * 5,
        1_000_000,
        3_000_000,
        [pltpu.VMEM((2, OPS, 2, STOPW, MODES, MODES), F32), DMA((2, OPS))],
        out_specs=HBM,
    )(own, near_a, near_b, far_a, far_b)


def solution(mesh):
    in_specs = (
        P("mode", "space", None, None),
        P("mode", "space"),
        P(),
        P("space", None, None, None),
        P(),
        P(),
    )
    out_specs = P("space", None, None, None, None, "mode")
    return jax.shard_map(
        per_device, mesh=mesh, in_specs=in_specs, out_specs=out_specs, check_vma=False
    )
```

```python
import functools
import math

import jax
import jax.numpy as jnp
from jax import lax
from jax.experimental import pallas as pl
from jax.experimental.pallas import tpu as pltpu
from jax.sharding import PartitionSpec as P

LAT = 64
STOPW = 7
PLANES = 8
SPOTS = 8
ITEMS = 64
WIDTH = 256
MODES = 32
ROWS = STOPW * MODES
COLS = 768
OPS = 4
CAND = 128
Z_GROUPS = [[z * SPOTS + p for z in range(PLANES)] for p in range(SPOTS)]
P_GROUPS = [[z * SPOTS + p for p in range(SPOTS)] for z in range(PLANES)]
PAIRS = [(0, 1), (3, 4), (6, 7), (9, 10), (2, 5), (8, 11)]
BF16 = jnp.bfloat16
F32 = jnp.float32


def iota(shape, axis):
    return lax.broadcasted_iota(jnp.int32, shape, axis)


def pack_kernel(route_ref, coefs_ref, counts_ref, out_ref):
    me = lax.axis_index("mode")
    row = route_ref[pl.ds(me // 2, 1), :]
    row = jnp.where(me % 2 == 1, pltpu.roll(row, 64, 1), row)[:, :ITEMS]
    owner = lax.shift_right_logical(row, 6)
    i = iota((ITEMS, ITEMS), 0)
    j = iota((ITEMS, ITEMS), 1)
    owners = jnp.broadcast_to(owner, (ITEMS, ITEMS)).astype(F32)
    column = jnp.sum(jnp.where(i == j, owners, 0.0), axis=1, keepdims=True)
    earlier = jnp.where((owners == column) & (i < j), 1.0, 0.0)
    rank = jnp.max(earlier, axis=0, keepdims=True).astype(jnp.int32)
    target = owner * 2 + rank
    q = iota((PLANES * 32, ITEMS), 0)
    plane = (lax.shift_right_logical(q, 5) - (lax.shift_right_logical(q, 4) & 1)) & 7
    want = plane * 16 + (q & 15)
    outgoing = jnp.where(want == target, 1.0, 0.0).astype(BF16)
    counts = jnp.broadcast_to(counts_ref[...], (ITEMS, ITEMS)).astype(F32)
    limit = jnp.sum(jnp.where(i == j, counts, 0.0), axis=1, keepdims=True).astype(jnp.int32)
    keep = iota((ITEMS, WIDTH), 1) < limit
    for part in range(2):
        block = jnp.where(keep, coefs_ref[:, part, :].astype(F32), 0.0).astype(BF16)
        packed = jnp.dot(outgoing, block, preferred_element_type=F32)
        out_ref[:, part * WIDTH : (part + 1) * WIDTH] = packed.astype(BF16)


def forward_kernel(got_ref, done_ref, out_ref, sorted_ref, sems):
    got = got_ref[...]
    copies = []
    for low, high, spots in ((112, 224, (0,)), (48, 112, (1, 2, 3, 4)), (0, 48, (5, 6, 7))):
        row = low + iota((high - low, PLANES * 32), 0)
        col = iota((high - low, PLANES * 32), 1)
        block = (SPOTS - 1 - lax.shift_right_logical(row, 4)) & 15
        source = (lax.shift_right_logical(row, 1) & 7) * 32 + block * 2 + (row & 1)
        order = jnp.where(col == source, 1.0, 0.0).astype(BF16)
        sorted_ref[low:high] = jnp.dot(order, got, preferred_element_type=F32).astype(BF16)
        for spot in spots:
            at = (SPOTS - 1 - spot) * 16
            copy = pltpu.make_async_copy(sorted_ref.at[at : at + STOPW * 16], out_ref.at[spot], sems.at[spot])
            copy.start()
            copies.append(copy)
    for copy in copies:
        copy.wait()


def tables_kernel(momenta_ref, gammas_ref, route_ref, after_ref, placer_ref, table_ref):
    me = lax.axis_index("mode")
    route = route_ref[...]
    owner = lax.shift_right_logical(route, 6)
    key = iota(route.shape, 0) * ITEMS + (route & (ITEMS - 1))
    keyf = key.astype(F32)
    second = (iota((1, CAND), 1) & 1) == 1
    mode = iota((MODES, CAND), 0)
    for stop in range(STOPW):
        hit = owner == ((me - stop) & 63)
        low = jnp.min(jnp.where(hit, keyf, 8192.0), axis=0, keepdims=True)
        high = jnp.max(jnp.where(hit, keyf, -1.0), axis=0, keepdims=True)
        valid = jnp.where(second, high - low, 8000.0 - low) > 0.0
        item = jnp.where(second, high, low).astype(jnp.int32) & (ITEMS - 1)
        item = jnp.where(valid, item, -1)
        for block in range(2):
            placer_ref[block, stop] = jnp.where(mode * 2 + block == item, 1.0, 0.0).astype(BF16)
    place = lax.axis_index("space")
    lane = iota((1, 128), 1)
    site = place * 64 + (lane & 63)
    xs = site & 3
    ys = lax.shift_right_logical(site, 2) & 3
    zs = lax.shift_right_logical(site, 4)
    for op in range(OPS):
        inner = momenta_ref[op, 0] * xs + momenta_ref[op, 1] * ys + momenta_ref[op, 2] * zs
        turn = inner.astype(F32) * (2.0 * math.pi / LAT)
        cosine = jnp.cos(turn)
        sine = jnp.sin(turn)
        bits = lax.shift_right_logical(gammas_ref[op], 2)
        for flag in range(2):
            at = OPS * 12 + op * 2 + flag
            on = lax.shift_right_logical(gammas_ref[op], flag) & 1
            table_ref[at : at + 1, :] = jnp.full((1, 128), on, jnp.int32).astype(F32)
        for group in range(6):
            spin = jnp.full((1, 128), group, jnp.int32) if group < 4 else 2 * (group - 4) + lax.shift_right_logical(lane, 6)
            common = spin & bits
            parity = (common ^ lax.shift_right_logical(common, 1)) & 1
            sign = (1 - 2 * parity).astype(F32)
            at = (op * 6 + group) * 2
            table_ref[at : at + 1, :] = cosine * sign
            table_ref[at + 1 : at + 2, :] = sine * sign


def block_of(mask):
    return lax.shift_right_logical(lax.axis_index("space") ^ mask, 1)


def sort_kernel(mask, basis_ref, *rest):
    far_ref, near_ref, done_ref, reads_ref, in_sems, done_sem = rest[-6:]
    step = 128
    chunks = 2 * WIDTH // step
    low = iota((step, 128), 1) < 64
    block = block_of(mask)
    core = lax.axis_index("space") & 1
    reads = []
    for chunk in range(chunks):
        rows = slice(chunk * step, (chunk + 1) * step)
        reads.append(pltpu.make_async_copy(basis_ref.at[block, rows, :], reads_ref.at[rows, :], in_sems.at[chunk]))
    for read in reads:
        read.start()
    for chunk, read in enumerate(reads):
        read.wait()
        if chunk == 0:
            done = pltpu.make_async_copy(reads_ref.at[:16, :128], done_ref, done_sem)
            done.start()
        rows = slice(chunk * step, (chunk + 1) * step)
        for out_ref, half in ((far_ref, 1 - core), (near_ref, core)):
            for group, (first, second) in enumerate(PAIRS):
                lanes = slice(group * 128, (group + 1) * 128)
                at = pl.multiple_of(half * 128, 128)
                a = reads_ref[rows, pl.ds(first * 256 + at, 128)]
                b = reads_ref[rows, pl.ds(second * 256 + at, 128)]
                out_ref[0, rows, lanes] = jnp.where(low, a, pltpu.roll(b, 64, 1))
                out_ref[1, rows, lanes] = jnp.where(low, pltpu.roll(a, 64, 1), b)
    done.wait()


def place(block, got_ref, placer_ref, coef_ref):
    for stop in range(STOPW):
        rows = got_ref[:, stop * 16 : (stop + 1) * 16, :].reshape(CAND, 2 * WIDTH)
        coef = jnp.dot(placer_ref[block, stop], rows, preferred_element_type=F32)
        re = coef[:, :WIDTH]
        im = coef[:, WIDTH:]
        top = slice(stop * MODES, (stop + 1) * MODES)
        bottom = slice(ROWS + stop * MODES, ROWS + (stop + 1) * MODES)
        coef_ref[top, :WIDTH] = re.astype(BF16)
        coef_ref[top, WIDTH:] = (-im).astype(BF16)
        coef_ref[bottom, :WIDTH] = im.astype(BF16)
        coef_ref[bottom, WIDTH:] = re.astype(BF16)


def expand(coef_ref, slab, vec_ref, chunk):
    lanes = slice(chunk * 256, (chunk + 1) * 256)
    vec = jnp.dot(coef_ref[...], slab[:, lanes], preferred_element_type=F32).astype(BF16)
    vec_ref[:, lanes] = vec[:ROWS]
    vec_ref[:, COLS + chunk * 256 : COLS + (chunk + 1) * 256] = vec[ROWS:]


def weigh(op, table_ref, vec_ref, weight_ref):
    at = OPS * 12 + op * 2
    swap = jnp.broadcast_to(table_ref[at : at + 1, :], (MODES, 128)) > 0.5
    cross = jnp.broadcast_to(table_ref[at + 1 : at + 2, :], (MODES, 128)) > 0.5
    spun = []
    for part in range(2):
        lanes = [slice(part * COLS + group * 128, part * COLS + (group + 1) * 128) for group in range(6)]
        v = [vec_ref[0:MODES, at].astype(F32) for at in lanes]
        r = [pltpu.roll(v[4 + half], 64, 1) for half in range(2)]
        crossed = [jnp.where(cross, v[spin ^ 2], v[spin]) for spin in range(4)]
        whole = [jnp.where(cross, v[4 + (half ^ 1)], v[4 + half]) for half in range(2)]
        turned = [jnp.where(cross, r[half ^ 1], r[half]) for half in range(2)]
        spun.append(
            [jnp.where(swap, crossed[spin ^ 1], crossed[spin]) for spin in range(4)]
            + [jnp.where(swap, turned[half], whole[half]) for half in range(2)]
        )
    for group in range(6):
        re = spun[0][group]
        im = spun[1][group]
        at = (op * 6 + group) * 2
        cosine = table_ref[at : at + 1, :]
        sine = table_ref[at + 1 : at + 2, :]
        w_re = cosine * re - sine * im
        w_im = sine * re + cosine * im
        real = slice(op * MODES, (op + 1) * MODES)
        imag = slice(128 + op * MODES, 128 + (op + 1) * MODES)
        left = slice(group * 128, (group + 1) * 128)
        right = slice(COLS + group * 128, COLS + (group + 1) * 128)
        weight_ref[real, left] = w_re.astype(BF16)
        weight_ref[real, right] = w_im.astype(BF16)
        weight_ref[imag, left] = (-w_im).astype(BF16)
        weight_ref[imag, right] = w_re.astype(BF16)


def contract(vec_ref, weight_ref, third):
    lanes = slice(third * 512, (third + 1) * 512)
    return lax.dot_general(
        vec_ref[:, lanes], weight_ref[:, lanes], (((1,), (1,)), ((), ())), preferred_element_type=F32
    )


def entries(table_ref, coef_ref, slab_ref, store, vec_0, weight_0, vec_1, weight_1):
    for chunk in range(3):
        expand(coef_ref, slab_ref[0], vec_0, chunk)
    for op in range(OPS):
        weigh(op, table_ref, vec_0, weight_0)
        if op < 3:
            expand(coef_ref, slab_ref[1], vec_1, op)
    total = None
    for op in range(OPS):
        if op < 3:
            part = contract(vec_0, weight_0, op)
            total = part if total is None else total + part
        weigh(op, table_ref, vec_1, weight_1)
    store(0, total)
    store(1, sum(contract(vec_1, weight_1, third) for third in range(3)))


def put(*refs):
    def store(t, total):
        refs[t][...] = total.astype(refs[t].dtype)

    return store


def first_kernel(mask, table_ref, got_ref, placer_ref, slab_ref, out_ref, coef_ref, *work):
    place(block_of(mask), got_ref, placer_ref, coef_ref)
    entries(table_ref, coef_ref, slab_ref, put(out_ref.at[0], out_ref.at[1]), *work)


def second_kernel(table_ref, coef_ref, slab_ref, out_ref, *work):
    entries(table_ref, coef_ref, slab_ref, put(out_ref.at[0], out_ref.at[1]), *work)


def pair_kernel(own_ref, other_ref, out_a_ref, out_b_ref):
    for t, out_ref in enumerate((out_a_ref, out_b_ref)):
        out_ref[...] = (own_ref[t] + other_ref[t].astype(F32)).astype(BF16)


def last_kernel(table_ref, got_ref, placer_ref, far_ref, near_ref, before_ref, part_a_ref, part_b_ref, own_ref, coef_ref, *work):
    place(block_of(0), got_ref, placer_ref, coef_ref)
    entries(table_ref, coef_ref, far_ref, put(part_a_ref, part_b_ref), *work)
    entries(table_ref, coef_ref, near_ref, put(own_ref.at[0], own_ref.at[1]), *work)


def total_kernel(own_ref, near_a_ref, near_b_ref, far_a_ref, far_b_ref, out_ref, total_ref, sems):
    copies = []
    for t, (near_ref, far_ref) in enumerate(((near_a_ref, far_a_ref), (near_b_ref, far_b_ref))):
        total = own_ref[t] + near_ref[...].astype(F32) + far_ref[...].astype(F32)
        for op in range(OPS):
            for r in range(2):
                at = (r * OPS + op) * MODES
                total_ref[t, op, r] = total[:, at : at + MODES].reshape(STOPW, MODES, MODES)
            copy = pltpu.make_async_copy(total_ref.at[t, op], out_ref.at[t, op], sems.at[t, op])
            copy.start()
            copies.append(copy)
    for copy in copies:
        copy.wait()


VMEM = pl.BlockSpec(memory_space=pltpu.VMEM)
SMEM = pl.BlockSpec(memory_space=pltpu.SMEM)
HBM = pl.BlockSpec(memory_space=pltpu.HBM)
DMA = pltpu.SemaphoreType.DMA


def kernel_call(kernel, out_shape, in_specs, flops, moved, scratch=(), limit=8, out_specs=None):
    many = isinstance(out_shape, tuple)
    return pl.pallas_call(
        kernel,
        out_shape=out_shape,
        in_specs=in_specs,
        out_specs=out_specs or ((VMEM,) * len(out_shape) if many else VMEM),
        scratch_shapes=list(scratch),
        compiler_params=pltpu.CompilerParams(vmem_limit_bytes=limit * 1024 * 1024),
        cost_estimate=pl.CostEstimate(flops=flops, bytes_accessed=moved, transcendentals=0),
    )


def shape(dims, dtype=BF16):
    return jax.ShapeDtypeStruct(dims, dtype)


def per_device(coefs, counts, route, basis, momenta, gammas):
    packed = kernel_call(
        pack_kernel, shape((PLANES * 32, 2 * WIDTH)), [VMEM] * 3, 20_000_000, 400_000, limit=60
    )(route.reshape(32, 128), coefs.reshape(ITEMS, 2, WIDTH), counts.reshape(1, ITEMS))
    first = lax.all_to_all(
        packed.reshape(PLANES, 32, 2 * WIDTH), "mode", 0, 0, tiled=True, axis_index_groups=Z_GROUPS
    )
    slab_shape = shape((2, 2 * WIDTH, COLS))
    token = shape((16, 128))

    def sort(mask, limit, *after):
        return kernel_call(
            functools.partial(sort_kernel, mask),
            (slab_shape, slab_shape, token),
            [HBM] * (1 + len(after)),
            5_000_000,
            6_000_000,
            [pltpu.VMEM((2 * WIDTH, 4 * COLS), BF16), DMA((4,)), DMA],
            limit=limit,
            out_specs=(VMEM, VMEM, HBM),
        )(basis.reshape(2, 2 * WIDTH, 4 * COLS), *after)

    slab_3, slab_2, done = sort(2, 52)
    onward = kernel_call(
        forward_kernel,
        shape((SPOTS, STOPW * 16, 2 * WIDTH)),
        [VMEM, HBM],
        70_000_000,
        1_200_000,
        [pltpu.VMEM(((SPOTS + STOPW - 1) * 16, 2 * WIDTH), BF16), DMA((SPOTS,))],
        out_specs=HBM,
    )(first.reshape(PLANES * 32, 2 * WIDTH), done)
    by_reader = route.reshape(PLANES, SPOTS, ITEMS).transpose(2, 1, 0).reshape(ITEMS, 64)
    by_reader = jnp.repeat(by_reader, 2, axis=1)
    placer, table = kernel_call(
        tables_kernel,
        (shape((2, STOPW, MODES, CAND)), shape((OPS * 14, 128), F32)),
        [SMEM, SMEM, VMEM, HBM],
        2_000_000,
        200_000,
    )(momenta, gammas, by_reader, onward)
    got = lax.all_to_all(onward, "mode", 0, 0, tiled=True, axis_index_groups=P_GROUPS)
    slab_1, slab_0, _ = sort(0, 59, onward)
    got, slab_1, slab_0 = lax.optimization_barrier((got, slab_1, slab_0))
    part_shape = shape((ROWS, 256))
    pair_shape = shape((2, ROWS, 256))
    wide_shape = shape((2, ROWS, 256), F32)
    coef_shape = (2 * ROWS, 2 * WIDTH)
    work = [pltpu.VMEM((ROWS, 2 * COLS), BF16), pltpu.VMEM((256, 2 * COLS), BF16)] * 2

    def between(pair, part):
        return lax.ppermute(part, "space", [(i, i ^ pair) for i in range(4)])

    part_3, coef = kernel_call(
        functools.partial(first_kernel, 3),
        (pair_shape, shape(coef_shape)),
        [VMEM] * 4,
        1_200_000_000,
        3_000_000,
        work,
    )(table, got, placer, slab_3)
    part_2 = kernel_call(second_kernel, wide_shape, [VMEM] * 3, 1_100_000_000, 3_000_000, work)(table, coef, slab_2)
    chip_a, chip_b = kernel_call(pair_kernel, (part_shape, part_shape), [VMEM] * 2, 200_000, 900_000)(
        part_2, between(1, part_3)
    )
    far_a = between(2, chip_a)
    far_b = between(2, chip_b)
    part_a, part_b, own = kernel_call(
        last_kernel,
        (part_shape, part_shape, wide_shape),
        [VMEM] * 6,
        2_200_000_000,
        6_000_000,
        [pltpu.VMEM(coef_shape, BF16)] + work,
    )(table, got, placer, slab_1, slab_0, chip_b)
    part_a, part_b, far_a = lax.optimization_barrier((part_a, part_b, far_a))
    near_a = between(1, part_a)
    near_b = between(1, part_b)
    return kernel_call(
        total_kernel,
        shape((2, OPS, 2, STOPW, MODES, MODES), F32),
        [VMEM] * 5,
        1_000_000,
        3_000_000,
        [pltpu.VMEM((2, OPS, 2, STOPW, MODES, MODES), F32), DMA((2, OPS))],
        out_specs=HBM,
    )(own, near_a, near_b, far_a, far_b)


def solution(mesh):
    in_specs = (
        P("mode", "space", None, None),
        P("mode", "space"),
        P(),
        P("space", None, None, None),
        P(),
        P(),
    )
    out_specs = P("space", None, None, None, None, "mode")
    return jax.shard_map(
        per_device, mesh=mesh, in_specs=in_specs, out_specs=out_specs, check_vma=False
    )
```

```python
import functools
import math

import jax
import jax.numpy as jnp
from jax import lax
from jax.experimental import pallas as pl
from jax.experimental.pallas import tpu as pltpu
from jax.sharding import PartitionSpec as P

LAT = 64
STOPW = 7
PLANES = 8
SPOTS = 8
ITEMS = 64
WIDTH = 256
MODES = 32
ROWS = STOPW * MODES
COLS = 768
OPS = 4
CAND = 128
Z_GROUPS = [[z * SPOTS + p for z in range(PLANES)] for p in range(SPOTS)]
P_GROUPS = [[z * SPOTS + p for p in range(SPOTS)] for z in range(PLANES)]
PAIRS = [(0, 1), (3, 4), (6, 7), (9, 10), (2, 5), (8, 11)]
BF16 = jnp.bfloat16
F32 = jnp.float32


def iota(shape, axis):
    return lax.broadcasted_iota(jnp.int32, shape, axis)


def pack_kernel(route_ref, coefs_ref, counts_ref, out_hbm, out_ref, sems):
    me = lax.axis_index("mode")
    row = route_ref[pl.ds(me // 2, 1), :]
    row = jnp.where(me % 2 == 1, pltpu.roll(row, 64, 1), row)[:, :ITEMS]
    owner = lax.shift_right_logical(row, 6)
    i = iota((ITEMS, ITEMS), 0)
    j = iota((ITEMS, ITEMS), 1)
    owners = jnp.broadcast_to(owner, (ITEMS, ITEMS)).astype(F32)
    column = jnp.sum(jnp.where(i == j, owners, 0.0), axis=1, keepdims=True)
    earlier = jnp.where((owners == column) & (i < j), 1.0, 0.0)
    rank = jnp.max(earlier, axis=0, keepdims=True).astype(jnp.int32)
    target = owner * 2 + rank
    q = iota((PLANES * 32, ITEMS), 0)
    plane = (lax.shift_right_logical(q, 5) - (lax.shift_right_logical(q, 4) & 1)) & 7
    want = plane * 16 + (q & 15)
    outgoing = jnp.where(want == target, 1.0, 0.0).astype(BF16)
    counts = jnp.broadcast_to(counts_ref[...], (ITEMS, ITEMS)).astype(F32)
    limit = jnp.sum(jnp.where(i == j, counts, 0.0), axis=1, keepdims=True).astype(jnp.int32)
    keep = iota((ITEMS, WIDTH), 1) < limit
    blocks = [jnp.where(keep, coefs_ref[:, part, :].astype(F32), 0.0).astype(BF16) for part in range(2)]
    writes = []
    for half in range(2):
        rows = slice(half * 128, (half + 1) * 128)
        for part in range(2):
            packed = jnp.dot(outgoing[rows], blocks[part], preferred_element_type=F32)
            out_ref[rows, part * WIDTH : (part + 1) * WIDTH] = packed.astype(BF16)
        write = pltpu.make_async_copy(out_ref.at[rows], out_hbm.at[rows], sems.at[half])
        write.start()
        writes.append(write)
    for write in writes:
        write.wait()


def forward_kernel(got_ref, done_ref, out_ref, sorted_ref, sems):
    got = got_ref[...]
    copies = []
    for low, high, spots in ((112, 224, (0,)), (48, 112, (1, 2, 3, 4)), (0, 48, (5, 6, 7))):
        row = low + iota((high - low, PLANES * 32), 0)
        col = iota((high - low, PLANES * 32), 1)
        block = (SPOTS - 1 - lax.shift_right_logical(row, 4)) & 15
        source = (lax.shift_right_logical(row, 1) & 7) * 32 + block * 2 + (row & 1)
        order = jnp.where(col == source, 1.0, 0.0).astype(BF16)
        sorted_ref[low:high] = jnp.dot(order, got, preferred_element_type=F32).astype(BF16)
        for spot in spots:
            at = (SPOTS - 1 - spot) * 16
            copy = pltpu.make_async_copy(sorted_ref.at[at : at + STOPW * 16], out_ref.at[spot], sems.at[spot])
            copy.start()
            copies.append(copy)
    for copy in copies:
        copy.wait()


def tables_kernel(momenta_ref, gammas_ref, route_ref, after_ref, placer_ref, table_ref):
    me = lax.axis_index("mode")
    route = route_ref[...]
    owner = lax.shift_right_logical(route, 6)
    key = iota(route.shape, 0) * ITEMS + (route & (ITEMS - 1))
    keyf = key.astype(F32)
    second = (iota((1, CAND), 1) & 1) == 1
    mode = iota((MODES, CAND), 0)
    for stop in range(STOPW):
        hit = owner == ((me - stop) & 63)
        low = jnp.min(jnp.where(hit, keyf, 8192.0), axis=0, keepdims=True)
        high = jnp.max(jnp.where(hit, keyf, -1.0), axis=0, keepdims=True)
        valid = jnp.where(second, high - low, 8000.0 - low) > 0.0
        item = jnp.where(second, high, low).astype(jnp.int32) & (ITEMS - 1)
        item = jnp.where(valid, item, -1)
        for block in range(2):
            placer_ref[block, stop] = jnp.where(mode * 2 + block == item, 1.0, 0.0).astype(BF16)
    place = lax.axis_index("space")
    lane = iota((1, 128), 1)
    site = place * 64 + (lane & 63)
    xs = site & 3
    ys = lax.shift_right_logical(site, 2) & 3
    zs = lax.shift_right_logical(site, 4)
    for op in range(OPS):
        inner = momenta_ref[op, 0] * xs + momenta_ref[op, 1] * ys + momenta_ref[op, 2] * zs
        turn = inner.astype(F32) * (2.0 * math.pi / LAT)
        cosine = jnp.cos(turn)
        sine = jnp.sin(turn)
        bits = lax.shift_right_logical(gammas_ref[op], 2)
        for flag in range(2):
            at = OPS * 12 + op * 2 + flag
            on = lax.shift_right_logical(gammas_ref[op], flag) & 1
            table_ref[at : at + 1, :] = jnp.full((1, 128), on, jnp.int32).astype(F32)
        for group in range(6):
            spin = jnp.full((1, 128), group, jnp.int32) if group < 4 else 2 * (group - 4) + lax.shift_right_logical(lane, 6)
            common = spin & bits
            parity = (common ^ lax.shift_right_logical(common, 1)) & 1
            sign = (1 - 2 * parity).astype(F32)
            at = (op * 6 + group) * 2
            table_ref[at : at + 1, :] = cosine * sign
            table_ref[at + 1 : at + 2, :] = sine * sign


def block_of(mask):
    return lax.shift_right_logical(lax.axis_index("space") ^ mask, 1)


def sort_kernel(mask, basis_ref, *rest):
    far_ref, near_ref, done_ref, reads_ref, in_sems, done_sem = rest[-6:]
    step = 128
    chunks = 2 * WIDTH // step
    low = iota((step, 128), 1) < 64
    block = block_of(mask)
    core = lax.axis_index("space") & 1
    reads = []
    for chunk in range(chunks):
        rows = slice(chunk * step, (chunk + 1) * step)
        reads.append(pltpu.make_async_copy(basis_ref.at[block, rows, :], reads_ref.at[rows, :], in_sems.at[chunk]))
    for read in reads:
        read.start()
    for chunk, read in enumerate(reads):
        read.wait()
        if chunk == 0:
            done = pltpu.make_async_copy(reads_ref.at[:16, :128], done_ref, done_sem)
            done.start()
        rows = slice(chunk * step, (chunk + 1) * step)
        for out_ref, half in ((far_ref, 1 - core), (near_ref, core)):
            for group, (first, second) in enumerate(PAIRS):
                lanes = slice(group * 128, (group + 1) * 128)
                at = pl.multiple_of(half * 128, 128)
                a = reads_ref[rows, pl.ds(first * 256 + at, 128)]
                b = reads_ref[rows, pl.ds(second * 256 + at, 128)]
                out_ref[0, rows, lanes] = jnp.where(low, a, pltpu.roll(b, 64, 1))
                out_ref[1, rows, lanes] = jnp.where(low, pltpu.roll(a, 64, 1), b)
    done.wait()


def place(block, got_ref, placer_ref, coef_ref):
    for stop in range(STOPW):
        rows = got_ref[:, stop * 16 : (stop + 1) * 16, :].reshape(CAND, 2 * WIDTH)
        coef = jnp.dot(placer_ref[block, stop], rows, preferred_element_type=F32)
        re = coef[:, :WIDTH]
        im = coef[:, WIDTH:]
        top = slice(stop * MODES, (stop + 1) * MODES)
        bottom = slice(ROWS + stop * MODES, ROWS + (stop + 1) * MODES)
        coef_ref[top, :WIDTH] = re.astype(BF16)
        coef_ref[top, WIDTH:] = (-im).astype(BF16)
        coef_ref[bottom, :WIDTH] = im.astype(BF16)
        coef_ref[bottom, WIDTH:] = re.astype(BF16)


def expand(coef_ref, slab, vec_ref, chunk):
    lanes = slice(chunk * 256, (chunk + 1) * 256)
    vec = jnp.dot(coef_ref[...], slab[:, lanes], preferred_element_type=F32).astype(BF16)
    vec_ref[:, lanes] = vec[:ROWS]
    vec_ref[:, COLS + chunk * 256 : COLS + (chunk + 1) * 256] = vec[ROWS:]


def weigh(op, table_ref, vec_ref, weight_ref):
    at = OPS * 12 + op * 2
    swap = jnp.broadcast_to(table_ref[at : at + 1, :], (MODES, 128)) > 0.5
    cross = jnp.broadcast_to(table_ref[at + 1 : at + 2, :], (MODES, 128)) > 0.5
    spun = []
    for part in range(2):
        lanes = [slice(part * COLS + group * 128, part * COLS + (group + 1) * 128) for group in range(6)]
        v = [vec_ref[0:MODES, at].astype(F32) for at in lanes]
        r = [pltpu.roll(v[4 + half], 64, 1) for half in range(2)]
        crossed = [jnp.where(cross, v[spin ^ 2], v[spin]) for spin in range(4)]
        whole = [jnp.where(cross, v[4 + (half ^ 1)], v[4 + half]) for half in range(2)]
        turned = [jnp.where(cross, r[half ^ 1], r[half]) for half in range(2)]
        spun.append(
            [jnp.where(swap, crossed[spin ^ 1], crossed[spin]) for spin in range(4)]
            + [jnp.where(swap, turned[half], whole[half]) for half in range(2)]
        )
    for group in range(6):
        re = spun[0][group]
        im = spun[1][group]
        at = (op * 6 + group) * 2
        cosine = table_ref[at : at + 1, :]
        sine = table_ref[at + 1 : at + 2, :]
        w_re = cosine * re - sine * im
        w_im = sine * re + cosine * im
        real = slice(op * MODES, (op + 1) * MODES)
        imag = slice(128 + op * MODES, 128 + (op + 1) * MODES)
        left = slice(group * 128, (group + 1) * 128)
        right = slice(COLS + group * 128, COLS + (group + 1) * 128)
        weight_ref[real, left] = w_re.astype(BF16)
        weight_ref[real, right] = w_im.astype(BF16)
        weight_ref[imag, left] = (-w_im).astype(BF16)
        weight_ref[imag, right] = w_re.astype(BF16)


def contract(vec_ref, weight_ref, third):
    lanes = slice(third * 512, (third + 1) * 512)
    return lax.dot_general(
        vec_ref[:, lanes], weight_ref[:, lanes], (((1,), (1,)), ((), ())), preferred_element_type=F32
    )


def entries(table_ref, coef_ref, slab_ref, store, vec_0, weight_0, vec_1, weight_1):
    for chunk in range(3):
        expand(coef_ref, slab_ref[0], vec_0, chunk)
    for op in range(OPS):
        weigh(op, table_ref, vec_0, weight_0)
        if op < 3:
            expand(coef_ref, slab_ref[1], vec_1, op)
    total = None
    for op in range(OPS):
        if op < 3:
            part = contract(vec_0, weight_0, op)
            total = part if total is None else total + part
        weigh(op, table_ref, vec_1, weight_1)
    store(0, total)
    store(1, sum(contract(vec_1, weight_1, third) for third in range(3)))


def put(*refs):
    def store(t, total):
        refs[t][...] = total.astype(refs[t].dtype)

    return store


def first_kernel(mask, table_ref, got_ref, placer_ref, slab_ref, out_ref, coef_ref, *work):
    place(block_of(mask), got_ref, placer_ref, coef_ref)
    entries(table_ref, coef_ref, slab_ref, put(out_ref.at[0], out_ref.at[1]), *work)


def second_kernel(table_ref, coef_ref, slab_ref, out_ref, *work):
    entries(table_ref, coef_ref, slab_ref, put(out_ref.at[0], out_ref.at[1]), *work)


def pair_kernel(own_ref, other_ref, out_a_ref, out_b_ref):
    for t, out_ref in enumerate((out_a_ref, out_b_ref)):
        out_ref[...] = (own_ref[t] + other_ref[t].astype(F32)).astype(BF16)


def last_kernel(table_ref, got_ref, placer_ref, far_ref, near_ref, before_ref, part_a_ref, part_b_ref, own_ref, coef_ref, *work):
    place(block_of(0), got_ref, placer_ref, coef_ref)
    entries(table_ref, coef_ref, far_ref, put(part_a_ref, part_b_ref), *work)
    entries(table_ref, coef_ref, near_ref, put(own_ref.at[0], own_ref.at[1]), *work)


def total_kernel(own_ref, near_a_ref, near_b_ref, far_a_ref, far_b_ref, out_ref, total_ref, sems):
    copies = []
    for t, (near_ref, far_ref) in enumerate(((near_a_ref, far_a_ref), (near_b_ref, far_b_ref))):
        total = own_ref[t] + near_ref[...].astype(F32) + far_ref[...].astype(F32)
        for op in range(OPS):
            for r in range(2):
                at = (r * OPS + op) * MODES
                total_ref[t, op, r] = total[:, at : at + MODES].reshape(STOPW, MODES, MODES)
            copy = pltpu.make_async_copy(total_ref.at[t, op], out_ref.at[t, op], sems.at[t, op])
            copy.start()
            copies.append(copy)
    for copy in copies:
        copy.wait()


VMEM = pl.BlockSpec(memory_space=pltpu.VMEM)
SMEM = pl.BlockSpec(memory_space=pltpu.SMEM)
HBM = pl.BlockSpec(memory_space=pltpu.HBM)
DMA = pltpu.SemaphoreType.DMA


def kernel_call(kernel, out_shape, in_specs, flops, moved, scratch=(), limit=8, out_specs=None):
    many = isinstance(out_shape, tuple)
    return pl.pallas_call(
        kernel,
        out_shape=out_shape,
        in_specs=in_specs,
        out_specs=out_specs or ((VMEM,) * len(out_shape) if many else VMEM),
        scratch_shapes=list(scratch),
        compiler_params=pltpu.CompilerParams(vmem_limit_bytes=limit * 1024 * 1024),
        cost_estimate=pl.CostEstimate(flops=flops, bytes_accessed=moved, transcendentals=0),
    )


def shape(dims, dtype=BF16):
    return jax.ShapeDtypeStruct(dims, dtype)


def per_device(coefs, counts, route, basis, momenta, gammas):
    packed = kernel_call(
        pack_kernel,
        shape((PLANES * 32, 2 * WIDTH)),
        [VMEM] * 3,
        20_000_000,
        400_000,
        [pltpu.VMEM((PLANES * 32, 2 * WIDTH), BF16), DMA((2,))],
        limit=60,
        out_specs=HBM,
    )(route.reshape(32, 128), coefs.reshape(ITEMS, 2, WIDTH), counts.reshape(1, ITEMS))
    first = lax.all_to_all(
        packed.reshape(PLANES, 32, 2 * WIDTH), "mode", 0, 0, tiled=True, axis_index_groups=Z_GROUPS
    )
    slab_shape = shape((2, 2 * WIDTH, COLS))
    token = shape((16, 128))

    def sort(mask, limit, *after):
        return kernel_call(
            functools.partial(sort_kernel, mask),
            (slab_shape, slab_shape, token),
            [HBM] * (1 + len(after)),
            5_000_000,
            6_000_000,
            [pltpu.VMEM((2 * WIDTH, 4 * COLS), BF16), DMA((4,)), DMA],
            limit=limit,
            out_specs=(VMEM, VMEM, HBM),
        )(basis.reshape(2, 2 * WIDTH, 4 * COLS), *after)

    slab_3, slab_2, done = sort(2, 52)
    onward = kernel_call(
        forward_kernel,
        shape((SPOTS, STOPW * 16, 2 * WIDTH)),
        [VMEM, HBM],
        70_000_000,
        1_200_000,
        [pltpu.VMEM(((SPOTS + STOPW - 1) * 16, 2 * WIDTH), BF16), DMA((SPOTS,))],
        out_specs=HBM,
    )(first.reshape(PLANES * 32, 2 * WIDTH), done)
    by_reader = route.reshape(PLANES, SPOTS, ITEMS).transpose(2, 1, 0).reshape(ITEMS, 64)
    by_reader = jnp.repeat(by_reader, 2, axis=1)
    placer, table = kernel_call(
        tables_kernel,
        (shape((2, STOPW, MODES, CAND)), shape((OPS * 14, 128), F32)),
        [SMEM, SMEM, VMEM, HBM],
        2_000_000,
        200_000,
    )(momenta, gammas, by_reader, onward)
    got = lax.all_to_all(onward, "mode", 0, 0, tiled=True, axis_index_groups=P_GROUPS)
    slab_1, slab_0, _ = sort(0, 59, onward)
    got, slab_1, slab_0 = lax.optimization_barrier((got, slab_1, slab_0))
    part_shape = shape((ROWS, 256))
    pair_shape = shape((2, ROWS, 256))
    wide_shape = shape((2, ROWS, 256), F32)
    coef_shape = (2 * ROWS, 2 * WIDTH)
    work = [pltpu.VMEM((ROWS, 2 * COLS), BF16), pltpu.VMEM((256, 2 * COLS), BF16)] * 2

    def between(pair, part):
        return lax.ppermute(part, "space", [(i, i ^ pair) for i in range(4)])

    part_3, coef = kernel_call(
        functools.partial(first_kernel, 3),
        (pair_shape, shape(coef_shape)),
        [VMEM] * 4,
        1_200_000_000,
        3_000_000,
        work,
    )(table, got, placer, slab_3)
    part_2 = kernel_call(second_kernel, wide_shape, [VMEM] * 3, 1_100_000_000, 3_000_000, work)(table, coef, slab_2)
    chip_a, chip_b = kernel_call(pair_kernel, (part_shape, part_shape), [VMEM] * 2, 200_000, 900_000)(
        part_2, between(1, part_3)
    )
    far_a = between(2, chip_a)
    far_b = between(2, chip_b)
    part_a, part_b, own = kernel_call(
        last_kernel,
        (part_shape, part_shape, wide_shape),
        [VMEM] * 6,
        2_200_000_000,
        6_000_000,
        [pltpu.VMEM(coef_shape, BF16)] + work,
    )(table, got, placer, slab_1, slab_0, chip_b)
    part_a, part_b, far_a = lax.optimization_barrier((part_a, part_b, far_a))
    near_a = between(1, part_a)
    near_b = between(1, part_b)
    return kernel_call(
        total_kernel,
        shape((2, OPS, 2, STOPW, MODES, MODES), F32),
        [VMEM] * 5,
        1_000_000,
        3_000_000,
        [pltpu.VMEM((2, OPS, 2, STOPW, MODES, MODES), F32), DMA((2, OPS))],
        out_specs=HBM,
    )(own, near_a, near_b, far_a, far_b)


def solution(mesh):
    in_specs = (
        P("mode", "space", None, None),
        P("mode", "space"),
        P(),
        P("space", None, None, None),
        P(),
        P(),
    )
    out_specs = P("space", None, None, None, None, "mode")
    return jax.shard_map(
        per_device, mesh=mesh, in_specs=in_specs, out_specs=out_specs, check_vma=False
    )
```
